32 devices in a mesh: dp: 8 (over z, y), tensor: 4 (over x, core).
Axes of the slice: x: 2, y: 2, z: 4, core: 2. Of those that a mesh axis runs over, the one named last changes fastest.
Arguments:
- resid_in: float32 [16384, 1536], P(('dp', 'tensor')), may hold values from -6 to 6
- cotangent: float32 [16384, 1536], P(('dp', 'tensor')), may hold values from -6 to 6
- w_zx: float32 [2, 1536, 2, 3072], P(None, 'dp', None, 'tensor'), may hold values from -0.15625 to 0.15625
- w_bc: float32 [2, 1536, 256], P(None, ('dp', 'tensor')), may hold values from -0.15625 to 0.15625
- w_dt: float32 [2, 1536, 48], P(None, 'dp', 'tensor'), may hold values from -0.15625 to 0.15625
- w_out: float32 [2, 3072, 1536], P(None, 'tensor', 'dp'), may hold values from -0.109375 to 0.109375
- chan_par: float32 [2, 6, 3072], P(None, None, 'tensor'), may hold values from -2.4 to 2.4
- head_par: float32 [2, 3, 48], P(None, None, 'tensor'), may hold values from -6 to 1.5
- bc_par: float32 [2, 5, 256], P(None, None, ('dp', 'tensor')), may hold values from -0.8 to 0.8
- norm_gain: float32 [2, 1536], P(None, ('dp', 'tensor')), may hold values from 0.5 to 1.5
- zx_first: float32 [2, 1536, 2, 3072], P(None, 'dp', None, 'tensor'), as said below
- zx_second: float32 [2, 1536, 2, 3072], P(None, 'dp', None, 'tensor'), as said below
- bc_first: float32 [2, 1536, 256], P(None, ('dp', 'tensor')), as said below
- bc_second: float32 [2, 1536, 256], P(None, ('dp', 'tensor')), as said below
- dt_first: float32 [2, 1536, 48], P(None, 'dp', 'tensor'), as said below
- dt_second: float32 [2, 1536, 48], P(None, 'dp', 'tensor'), as said below
- out_first: float32 [2, 3072, 1536], P(None, 'tensor', 'dp'), as said below
- out_second: float32 [2, 3072, 1536], P(None, 'tensor', 'dp'), as said below
- chan_first: float32 [2, 6, 3072], P(None, None, 'tensor'), as said below
- chan_second: float32 [2, 6, 3072], P(None, None, 'tensor'), as said below
- head_first: float32 [2, 3, 48], P(None, None, 'tensor'), as said below
- head_second: float32 [2, 3, 48], P(None, None, 'tensor'), as said below
- bcpar_first: float32 [2, 5, 256], P(None, None, ('dp', 'tensor')), as said below
- bcpar_second: float32 [2, 5, 256], P(None, None, ('dp', 'tensor')), as said below
- gain_first: float32 [2, 1536], P(None, ('dp', 'tensor')), as said below
- gain_second: float32 [2, 1536], P(None, ('dp', 'tensor')), as said below
Outputs:
- resid_out: float32 [16384, 1536], P(('dp', 'tensor'))
- resid_grad: float32 [16384, 1536], P(('dp', 'tensor'))
- zx_updated: float32 [2, 1536, 2, 3072], P(None, 'dp', None, 'tensor')
- zx_first_new: float32 [2, 1536, 2, 3072], P(None, 'dp', None, 'tensor')
- zx_second_new: float32 [2, 1536, 2, 3072], P(None, 'dp', None, 'tensor')
- bc_updated: float32 [2, 1536, 256], P(None, ('dp', 'tensor'))
- bc_first_new: float32 [2, 1536, 256], P(None, ('dp', 'tensor'))
- bc_second_new: float32 [2, 1536, 256], P(None, ('dp', 'tensor'))
- dt_updated: float32 [2, 1536, 48], P(None, 'dp', 'tensor')
- dt_first_new: float32 [2, 1536, 48], P(None, 'dp', 'tensor')
- dt_second_new: float32 [2, 1536, 48], P(None, 'dp', 'tensor')
- out_updated: float32 [2, 3072, 1536], P(None, 'tensor', 'dp')
- out_first_new: float32 [2, 3072, 1536], P(None, 'tensor', 'dp')
- out_second_new: float32 [2, 3072, 1536], P(None, 'tensor', 'dp')
- chan_updated: float32 [2, 6, 3072], P(None, None, 'tensor')
- chan_first_new: float32 [2, 6, 3072], P(None, None, 'tensor')
- chan_second_new: float32 [2, 6, 3072], P(None, None, 'tensor')
- head_updated: float32 [2, 3, 48], P(None, None, 'tensor')
- head_first_new: float32 [2, 3, 48], P(None, None, 'tensor')
- head_second_new: float32 [2, 3, 48], P(None, None, 'tensor')
- bcpar_updated: float32 [2, 5, 256], P(None, None, ('dp', 'tensor'))
- bcpar_first_new: float32 [2, 5, 256], P(None, None, ('dp', 'tensor'))
- bcpar_second_new: float32 [2, 5, 256], P(None, None, ('dp', 'tensor'))
- gain_updated: float32 [2, 1536], P(None, ('dp', 'tensor'))
- gain_first_new: float32 [2, 1536], P(None, ('dp', 'tensor'))
- gain_second_new: float32 [2, 1536], P(None, ('dp', 'tensor'))
The draws below stay inside these ranges and needn't reach their ends.
Inputs may be any that keep to these rules, and one draw needn't show every extreme that they name: `zx_first`: of both signs. `zx_second`: positive. `bc_first`: of both signs. `bc_second`: positive. `dt_first`: of both signs. `dt_second`: positive. `out_first`: of both signs. `out_second`: positive. `chan_first`: of both signs. `chan_second`: positive. `head_first`: of both signs. `head_second`: positive. `bcpar_first`: of both signs. `bcpar_second`: positive. `gain_first`: of both signs. `gain_second`: positive.
All inputs are finite; a program needn't handle non-finite values.
Results may differ from the reference program's by a relative error of at most 0.01.
The reference program's roundings to bfloat16 on the way count: a program that leaves them out, or rounds other values in their place, can miss the bound.
Values may be sent and summed in bfloat16 or wider, within the bound.
No kernel may reach another device: no remote copies, remote signals or barrier semaphores. Data moves between devices by JAX's collectives and lax.ppermute only.
A program may use at most 320 MiB of HBM per device.

```python
import math
import jax
import jax.numpy as jnp
from jax import lax

D = 1536
HEADS = 48
STATE = 128
CONV = 4
BLOCK = 256
LAYERS = 2
STEP = 10
LENGTH = 2048
INNER = 3072
TOKENS = 16384


def state_draw(key, shape, grad_coef, power):
    grad_size = grad_coef * math.sqrt(TOKENS)
    if power == 1:
        return jax.random.uniform(key, shape, jnp.float32, -1.0, 1.0) * (math.sqrt(3.0) * grad_size / 9.0)
    spread = jax.random.uniform(key, shape, jnp.float32, 0.0, math.log(4.0))
    return jnp.exp(spread) * (grad_size * grad_size / 19.0)


def draw_chan_par(key, part):
    key = jax.random.fold_in(key, 11)
    subkeys = jax.random.split(key, 3)
    channel = jnp.arange(INNER, dtype=jnp.float32) / (INNER - 1)
    rising = 1.0 + 2.0 * channel
    tap_values = jax.random.uniform(subkeys[0], (LAYERS, CONV, INNER), jnp.float32, -0.8, 0.8) * rising[None, None, :]
    conv_bias = jax.random.uniform(subkeys[1], (LAYERS, 1, INNER), jnp.float32, -0.5, 0.5)
    norm_scale = jax.random.uniform(subkeys[2], (LAYERS, 1, INNER), jnp.float32, 0.5, 1.5)
    return jnp.concatenate([tap_values, conv_bias, norm_scale], axis=1)


def draw_head_par(key, part):
    key = jax.random.fold_in(key, 12)
    subkeys = jax.random.split(key, 3)
    step_bias = jax.random.uniform(subkeys[0], (LAYERS, 1, HEADS), jnp.float32, -6.0, -2.0)
    log_decay = jax.random.uniform(subkeys[1], (LAYERS, 1, HEADS), jnp.float32, 0.0, 1.5)
    skip_gain = jax.random.uniform(subkeys[2], (LAYERS, 1, HEADS), jnp.float32, 0.5, 1.5)
    return jnp.concatenate([step_bias, log_decay, skip_gain], axis=1)


def draw_bc_par(key, part):
    key = jax.random.fold_in(key, 13)
    subkeys = jax.random.split(key, 2)
    tap_values = jax.random.uniform(subkeys[0], (LAYERS, CONV, 2 * STATE), jnp.float32, -0.8, 0.8)
    conv_bias = jax.random.uniform(subkeys[1], (LAYERS, 1, 2 * STATE), jnp.float32, -0.5, 0.5)
    return jnp.concatenate([tap_values, conv_bias], axis=1)


def draw_zx_first(key, part):
    key = jax.random.fold_in(key, 21)
    return state_draw(key, (LAYERS, D, 2, INNER), 0.4, 1)


def draw_zx_second(key, part):
    key = jax.random.fold_in(key, 22)
    return state_draw(key, (LAYERS, D, 2, INNER), 0.4, 2)


def draw_bc_first(key, part):
    key = jax.random.fold_in(key, 23)
    return state_draw(key, (LAYERS, D, 2 * STATE), 1.5, 1)


def draw_bc_second(key, part):
    key = jax.random.fold_in(key, 24)
    return state_draw(key, (LAYERS, D, 2 * STATE), 1.5, 2)


def draw_dt_first(key, part):
    key = jax.random.fold_in(key, 25)
    return state_draw(key, (LAYERS, D, HEADS), 0.4, 1)


def draw_dt_second(key, part):
    key = jax.random.fold_in(key, 26)
    return state_draw(key, (LAYERS, D, HEADS), 0.4, 2)


def draw_out_first(key, part):
    key = jax.random.fold_in(key, 27)
    return state_draw(key, (LAYERS, INNER, D), 1.0, 1)


def draw_out_second(key, part):
    key = jax.random.fold_in(key, 28)
    return state_draw(key, (LAYERS, INNER, D), 1.0, 2)


def draw_chan_first(key, part):
    key = jax.random.fold_in(key, 29)
    return state_draw(key, (LAYERS, CONV + 2, INNER), 0.5, 1)


def draw_chan_second(key, part):
    key = jax.random.fold_in(key, 30)
    return state_draw(key, (LAYERS, CONV + 2, INNER), 0.5, 2)


def draw_head_first(key, part):
    key = jax.random.fold_in(key, 31)
    return state_draw(key, (LAYERS, 3, HEADS), 1.5, 1)


def draw_head_second(key, part):
    key = jax.random.fold_in(key, 32)
    return state_draw(key, (LAYERS, 3, HEADS), 1.5, 2)


def draw_bcpar_first(key, part):
    key = jax.random.fold_in(key, 33)
    return state_draw(key, (LAYERS, CONV + 1, 2 * STATE), 1.5, 1)


def draw_bcpar_second(key, part):
    key = jax.random.fold_in(key, 34)
    return state_draw(key, (LAYERS, CONV + 1, 2 * STATE), 1.5, 2)


def draw_gain_first(key, part):
    key = jax.random.fold_in(key, 35)
    return state_draw(key, (LAYERS, D), 0.5, 1)


def draw_gain_second(key, part):
    key = jax.random.fold_in(key, 36)
    return state_draw(key, (LAYERS, D), 0.5, 2)


def block_scale(stream_key, extent, cuts, low, largest):
    def one(dim, blocks):
        draws = jax.random.uniform(jax.random.fold_in(jax.random.fold_in(stream_key, 6), dim), (blocks,), jnp.float32, low / len(cuts), largest / len(cuts))
        return jnp.repeat(jnp.exp(draws), extent[dim] // blocks).reshape((-1,) + (1,) * (len(extent) - dim - 1))

    gain = one(*cuts[0])
    for cut in cuts[1:]:
        gain = gain * one(*cut)
    return gain


def centred(stream_key, dims, scale, most, cuts=(), held_as=jnp.bfloat16):
    array = jax.random.normal(stream_key, dims, jnp.float32) * scale
    if len(cuts) > 0:
        array = block_scale(stream_key, dims, cuts, -0.22, 0.18) * array
    return jnp.clip(array, min=-most, max=most).astype(held_as)


def setup_inputs(seed: int = 0) -> dict:
    key_of = jax.random.split(jax.random.key(seed), 27)
    resid_in = centred(key_of[0], (TOKENS, D), 1.0, 6.0, ((0, 32),), jnp.float32)
    cotangent = centred(key_of[1], (TOKENS, D), 1.0, 6.0, ((0, 32),), jnp.float32)
    w_zx = centred(key_of[2], (LAYERS, D, 2, INNER), D ** -0.5, 0.15625, ((1, 8), (3, 4)), jnp.float32)
    w_bc = centred(key_of[3], (LAYERS, D, 2 * STATE), D ** -0.5, 0.15625, ((1, 32),), jnp.float32)
    w_dt = centred(key_of[4], (LAYERS, D, HEADS), D ** -0.5, 0.15625, ((1, 8), (2, 4)), jnp.float32)
    w_out = centred(key_of[5], (LAYERS, INNER, D), INNER ** -0.5, 0.109375, ((1, 4), (2, 8)), jnp.float32)
    chan_par = draw_chan_par(jax.random.fold_in(key_of[26], 71), 0)
    head_par = draw_head_par(jax.random.fold_in(key_of[26], 71), 0)
    bc_par = draw_bc_par(jax.random.fold_in(key_of[26], 71), 0)
    norm_gain = jnp.clip(1.0 + 0.1 * jax.random.normal(key_of[9], (LAYERS, D), jnp.float32), 0.5, 1.5)
    zx_first = draw_zx_first(jax.random.fold_in(key_of[26], 71), 0)
    zx_second = draw_zx_second(jax.random.fold_in(key_of[26], 71), 0)
    bc_first = draw_bc_first(jax.random.fold_in(key_of[26], 71), 0)
    bc_second = draw_bc_second(jax.random.fold_in(key_of[26], 71), 0)
    dt_first = draw_dt_first(jax.random.fold_in(key_of[26], 71), 0)
    dt_second = draw_dt_second(jax.random.fold_in(key_of[26], 71), 0)
    out_first = draw_out_first(jax.random.fold_in(key_of[26], 71), 0)
    out_second = draw_out_second(jax.random.fold_in(key_of[26], 71), 0)
    chan_first = draw_chan_first(jax.random.fold_in(key_of[26], 71), 0)
    chan_second = draw_chan_second(jax.random.fold_in(key_of[26], 71), 0)
    head_first = draw_head_first(jax.random.fold_in(key_of[26], 71), 0)
    head_second = draw_head_second(jax.random.fold_in(key_of[26], 71), 0)
    bcpar_first = draw_bcpar_first(jax.random.fold_in(key_of[26], 71), 0)
    bcpar_second = draw_bcpar_second(jax.random.fold_in(key_of[26], 71), 0)
    gain_first = draw_gain_first(jax.random.fold_in(key_of[26], 71), 0)
    gain_second = draw_gain_second(jax.random.fold_in(key_of[26], 71), 0)
    return {"resid_in": resid_in, "cotangent": cotangent, "w_zx": w_zx, "w_bc": w_bc, "w_dt": w_dt, "w_out": w_out, "chan_par": chan_par, "head_par": head_par, "bc_par": bc_par, "norm_gain": norm_gain, "zx_first": zx_first, "zx_second": zx_second, "bc_first": bc_first, "bc_second": bc_second, "dt_first": dt_first, "dt_second": dt_second, "out_first": out_first, "out_second": out_second, "chan_first": chan_first, "chan_second": chan_second, "head_first": head_first, "head_second": head_second, "bcpar_first": bcpar_first, "bcpar_second": bcpar_second, "gain_first": gain_first, "gain_second": gain_second}


NORM_EPS = 1e-05
BETA_ONE = 0.9
BETA_TWO = 0.95
ADAM_EPS = 1e-08
MATRIX_RATE = 0.02
MATRIX_DECAY = 0.1
SMALL_RATE = 0.3
HEAD_RATE = 2.0
PRECISE = lax.Precision.HIGHEST

@jax.custom_vjp
def low(v):
    return lax.optimization_barrier(v.astype(jnp.bfloat16)).astype(jnp.float32)

@jax.custom_vjp
def low_back(v):
    return v

def low_keep(v):
    return (low(v), None)

def low_pass(kept, grad):
    return (grad,)

def back_keep(v):
    return (v, None)

def back_low(kept, grad):
    return (low(grad),)
low.defvjp(low_keep, low_pass)
low_back.defvjp(back_keep, back_low)

def pre_norm(residual, gain_vals):
    return residual * lax.rsqrt(lax.optimization_barrier(jnp.mean(residual * residual, axis=1, keepdims=True)) + NORM_EPS) * gain_vals[None, :]

def causal_conv(values, tap_weights, conv_bias):
    tap_count = tap_weights.shape[0]
    padded = jnp.pad(values, ((tap_count - 1, 0), (0, 0)))
    summed = conv_bias[None, :] + tap_weights[tap_count - 1][None, :] * values
    for offset in range(tap_count - 1):
        summed = summed + tap_weights[offset][None, :] * padded[offset:offset + values.shape[0]]
    return summed

def block_step(carried_in, block_parts):
    old_state, decay_rate = carried_in
    block_x, block_dt, block_b, block_c = block_parts
    run_sum = jnp.cumsum(block_dt * decay_rate[None, :], axis=0).T
    positions = jnp.arange(block_dt.shape[0])
    causal = (positions[:, None] >= positions[None, :])[None, :, :]
    spread = jnp.where(causal, run_sum[:, :, None] - run_sum[:, None, :], 0.0)
    fading = jnp.where(causal, jnp.exp(spread), 0.0)
    affinity = jnp.dot(block_c, block_b.T, precision=PRECISE)
    mixing = affinity[None, :, :] * fading * block_dt.T[:, None, :]
    inside = jnp.einsum('hts,shp->thp', mixing, block_x, precision=PRECISE)
    from_state = jnp.exp(run_sum).T[:, :, None] * jnp.einsum('tn,hpn->thp', block_c, old_state, precision=PRECISE)
    tail_scale = jnp.exp(run_sum[:, -1:] - run_sum) * block_dt.T
    fresh = jnp.einsum('hs,shp,sn->hpn', tail_scale, block_x, block_b, precision=PRECISE)
    new_state = jnp.exp(run_sum[:, -1])[:, None, None] * old_state + fresh
    return ((new_state, decay_rate), inside + from_state)

def scan_blocks(inputs_x, step_dt, decay_rate, input_b, input_c):
    seq_len, head_count, head_width = inputs_x.shape
    block_count = seq_len // BLOCK
    block_parts = (inputs_x.reshape(block_count, BLOCK, head_count, head_width), step_dt.reshape(block_count, BLOCK, head_count), input_b.reshape(block_count, BLOCK, input_b.shape[1]), input_c.reshape(block_count, BLOCK, input_c.shape[1]))
    start_state = jnp.zeros((head_count, head_width, input_b.shape[1]), jnp.float32)
    final_carry, outputs = lax.scan(jax.checkpoint(block_step), (start_state, decay_rate), block_parts)
    return outputs.reshape(seq_len, head_count, head_width)

def mixer_local(proj_zx, proj_bc, proj_dt, chan_taps, head_vals, bc_vals):
    gate_z = proj_zx[:, 0, :]
    conv_x = jax.nn.silu(causal_conv(proj_zx[:, 1, :], chan_taps[:-1], chan_taps[-1]))
    conv_bc = jax.nn.silu(causal_conv(proj_bc, bc_vals[:-1], bc_vals[-1]))
    state_size = proj_bc.shape[1] // 2
    step_dt = jax.nn.softplus(proj_dt + head_vals[0][None, :])
    decay_rate = -jnp.exp(head_vals[1])
    head_count = proj_dt.shape[1]
    inputs_x = conv_x.reshape(conv_x.shape[0], head_count, conv_x.shape[1] // head_count)
    mixed = scan_blocks(inputs_x, step_dt, decay_rate, conv_bc[:, :state_size], conv_bc[:, state_size:])
    mixed = mixed + head_vals[2][None, :, None] * inputs_x
    gated_vals = mixed.reshape(conv_x.shape) * jax.nn.silu(gate_z)
    return (gated_vals, lax.optimization_barrier(jnp.sum(gated_vals * gated_vals, axis=1)))

def gated_norm(gated_vals, square_sum, norm_scale):
    return gated_vals * lax.rsqrt(square_sum[:, None] / INNER + NORM_EPS) * norm_scale[None, :]

def layer_sequence(residual, weights):
    zx_w, bc_w, dt_w, out_w, chan_vals, head_vals, bc_vals, gain_vals = weights
    normed = low(pre_norm(residual, gain_vals))
    proj_zx = low_back(jnp.einsum('td,dki->tki', normed, zx_w, precision=PRECISE))
    proj_bc = low_back(jnp.dot(normed, bc_w, precision=PRECISE))
    proj_dt = low_back(jnp.dot(normed, dt_w, precision=PRECISE))
    gated_vals, square_sum = mixer_local(proj_zx, proj_bc, proj_dt, chan_vals[:-1], head_vals, bc_vals)
    scaled = low(gated_norm(gated_vals, square_sum, chan_vals[-1]))
    branch = low_back(jnp.dot(scaled, out_w, precision=PRECISE))
    return residual + branch

def run_layer(hidden, weights):

    def apply_one(resid_seq):
        return jax.checkpoint(layer_sequence)(resid_seq, weights)
    return lax.map(apply_one, hidden)

def forward(resid_in, w_zx, w_bc, w_dt, w_out, chan_par, head_par, bc_par, norm_gain):
    hidden = resid_in.reshape(resid_in.shape[0] // LENGTH, LENGTH, resid_in.shape[1])
    for layer_index in range(LAYERS):
        weights = (low(w_zx[layer_index]), low(w_bc[layer_index]), low(w_dt[layer_index]), low(w_out[layer_index]), chan_par[layer_index], head_par[layer_index], bc_par[layer_index], norm_gain[layer_index])
        hidden = run_layer(hidden, weights)
    return hidden.reshape(resid_in.shape)

def adam_update(current, gradient, moment_old, square_old, step_rate, decay_coef):
    moment_new = BETA_ONE * moment_old + (1.0 - BETA_ONE) * gradient
    square_new = BETA_TWO * square_old + (1.0 - BETA_TWO) * gradient * gradient
    moment_hat = moment_new / (1.0 - BETA_ONE ** STEP)
    square_hat = square_new / (1.0 - BETA_TWO ** STEP)
    updated = current - step_rate * (moment_hat / (jnp.sqrt(square_hat) + ADAM_EPS) + decay_coef * current)
    return (updated, moment_new, square_new)

def reference(resid_in, cotangent, w_zx, w_bc, w_dt, w_out, chan_par, head_par, bc_par, norm_gain, zx_first, zx_second, bc_first, bc_second, dt_first, dt_second, out_first, out_second, chan_first, chan_second, head_first, head_second, bcpar_first, bcpar_second, gain_first, gain_second):
    resid_out, pull_back = jax.vjp(forward, resid_in, w_zx, w_bc, w_dt, w_out, chan_par, head_par, bc_par, norm_gain)
    grads_all = pull_back(cotangent)
    zx_updated, zx_first_new, zx_second_new = adam_update(w_zx, grads_all[1], zx_first, zx_second, MATRIX_RATE, MATRIX_DECAY)
    bc_updated, bc_first_new, bc_second_new = adam_update(w_bc, grads_all[2], bc_first, bc_second, MATRIX_RATE, MATRIX_DECAY)
    dt_updated, dt_first_new, dt_second_new = adam_update(w_dt, grads_all[3], dt_first, dt_second, MATRIX_RATE, MATRIX_DECAY)
    out_updated, out_first_new, out_second_new = adam_update(w_out, grads_all[4], out_first, out_second, MATRIX_RATE, MATRIX_DECAY)
    chan_updated, chan_first_new, chan_second_new = adam_update(chan_par, grads_all[5], chan_first, chan_second, SMALL_RATE, 0.0)
    head_updated, head_first_new, head_second_new = adam_update(head_par, grads_all[6], head_first, head_second, HEAD_RATE, 0.0)
    bcpar_updated, bcpar_first_new, bcpar_second_new = adam_update(bc_par, grads_all[7], bcpar_first, bcpar_second, SMALL_RATE, 0.0)
    gain_updated, gain_first_new, gain_second_new = adam_update(norm_gain, grads_all[8], gain_first, gain_second, SMALL_RATE, 0.0)
    return (resid_out, grads_all[0], zx_updated, zx_first_new, zx_second_new, bc_updated, bc_first_new, bc_second_new, dt_updated, dt_first_new, dt_second_new, out_updated, out_first_new, out_second_new, chan_updated, chan_first_new, chan_second_new, head_updated, head_first_new, head_second_new, bcpar_updated, bcpar_first_new, bcpar_second_new, gain_updated, gain_first_new, gain_second_new)
```

```python
import functools
import math

import jax
import jax.numpy as jnp
from jax import lax
from jax.experimental import pallas as pl
from jax.experimental.layout import Layout, with_layout_constraint
from jax.experimental.pallas import tpu as pltpu
from jax.sharding import PartitionSpec as P

BLOCK = 256
STEP = 10
INNER = 3072
LANES = 128
HEAD_WIDTH = 64

NORM_EPS = 1e-05
BETA_ONE = 0.9
BETA_TWO = 0.95
ADAM_EPS = 1e-08
MATRIX_RATE = 0.02
MATRIX_DECAY = 0.1
SMALL_RATE = 0.3
HEAD_RATE = 2.0
PRECISE = lax.Precision.HIGHEST
LOG2E = math.log2(math.e)
LOW = jnp.bfloat16
F32 = jnp.float32
VMEM_BYTES = 56 * 1024 * 1024


def dot(left, right, left_dim=1, right_dim=0, precision=None):
    return lax.dot_general(
        left,
        right,
        (((left_dim,), (right_dim,)), ((), ())),
        preferred_element_type=F32,
        precision=precision,
    )


def split(vals):
    high = vals.astype(LOW)
    return high, (vals - high.astype(F32)).astype(LOW)


def halves(vals):
    return jnp.concatenate(split(vals), axis=1)


def left_parts(vals, axis):
    high, low = split(vals)
    return jnp.concatenate([high, low, high], axis=axis)


def right_parts(vals, axis):
    high, low = split(vals)
    return jnp.concatenate([high, high, low], axis=axis)


def mix_pair(mixing, pair):
    out = dot(jnp.concatenate(split(mixing), axis=1), jnp.concatenate([pair, pair], axis=0))
    return out[:, :LANES] + out[:, LANES:]


def softplus(vals):
    return jnp.maximum(vals, 0.0) + jnp.log1p(jnp.exp(-jnp.abs(vals)))


def conv_block(ext, conv_ref):
    rows = ext.shape[0] - 8
    total = conv_ref[4:5, :] + conv_ref[3:4, :] * ext[8 : 8 + rows, :]
    for tap in range(3):
        total = total + conv_ref[tap : tap + 1, :] * ext[5 + tap : 5 + tap + rows, :]
    return total


def decay_sums(step_dt, head_ref):
    size = step_dt.shape[0]
    row = lax.broadcasted_iota(jnp.int32, (size, size), 0)
    col = lax.broadcasted_iota(jnp.int32, (size, size), 1)
    lower = jnp.where(row >= col, 1.0, 0.0).astype(F32)
    return dot(lower, step_dt * head_ref[1:2, :], precision=PRECISE)


def scan_kernel(
    me_ref, rows_ref, weight_ref, conv_ref, head_ref, skip_ref, spread_ref,
    pre_ref, y_ref, kept_ref, state, ext,
):
    width = y_ref.shape[1]
    conv_width = ext.shape[1]
    half = (conv_width - width) // 2
    size = rows_ref.shape[0]

    @pl.when(pl.program_id(0) == 0)
    def _():
        state[...] = jnp.zeros_like(state)
        ext[0:8, :] = jnp.zeros((8, conv_width), F32)

    @pl.when(pl.program_id(0) > 0)
    def _():
        ext[0:8, :] = ext[size : size + 8, :]

    pre = dot(rows_ref[...], weight_ref[...])
    pre_ref[...] = pre
    ext[8 : 8 + size, :] = pre[:, :conv_width]
    conv = conv_block(ext, conv_ref)
    act = conv * jax.nn.sigmoid(conv)
    inputs_x = act[:, :width]
    left_c = left_parts(act[:, width + half :], 1)
    step_dt = softplus(pre[:, conv_width:] + head_ref[0:1, :])
    cum = decay_sums(step_dt, head_ref)
    cum_t = cum.T
    last = cum[size - 1 : size, :]
    spread = spread_ref[...]
    dt_wide = dot(halves(step_dt), spread)
    cum_wide = dot(halves(jnp.exp2(cum)), spread)
    tail_wide = dot(halves(jnp.exp2(last - cum)), spread)
    scaled_x = inputs_x * dt_wide
    high_x, low_x = split(scaled_x)
    row = lax.broadcasted_iota(jnp.int32, (size, size), 0)
    col = lax.broadcasted_iota(jnp.int32, (size, size), 1)
    affinity = jnp.where(row >= col, dot(left_c, right_parts(act[:, width : width + half], 1), 1, 1), 0.0)
    old_state = state[...]
    kept_ref[0] = old_state
    y_ref[...] = (
        cum_wide * dot(left_c, right_parts(old_state, 0)) + skip_ref[0:1, :] * inputs_x
    )
    state[...] = cum_wide[size - 1 : size, :] * old_state + dot(
        left_parts(act[:, width : width + half], 0), right_parts(scaled_x * tail_wide, 0), 0, 0
    )
    first_half = lax.broadcasted_iota(jnp.int32, (size, LANES), 1) < HEAD_WIDTH
    for pair in range(width // LANES):
        cols = slice(pair * LANES, (pair + 1) * LANES)
        pair_x = jnp.concatenate([high_x[:, cols], low_x[:, cols]], axis=1)
        parts = []
        for head in (2 * pair, 2 * pair + 1):
            gap = cum[:, head : head + 1] - cum_t[head : head + 1, :]
            parts.append(mix_pair(affinity * jnp.exp2(jnp.minimum(gap, 0.0)), pair_x))
        y_ref[:, cols] += jnp.where(first_half, parts[0], parts[1])


def gate_kernel(rows_ref, y_ref, z_weight_ref, out_weight_ref, gain_ref, *refs):
    z_ref, sent_ref, own_ref, sq_ref = refs[-4:]
    gate_z = dot(rows_ref[...], z_weight_ref[...])
    z_ref[...] = gate_z
    gated = y_ref[...] * (gate_z * jax.nn.sigmoid(gate_z))
    sq_ref[...] = jnp.sum(gated * gated, axis=1, keepdims=True)
    low_gated = (gated * gain_ref[...]).astype(LOW)
    partial = dot(low_gated, out_weight_ref[...], 1, 1).astype(LOW)
    sending = pl.program_id(0) < pl.num_programs(0) // 2

    @pl.when(sending)
    def _():
        sent_ref[...] = partial

    @pl.when(jnp.logical_not(sending))
    def _():
        own_ref[...] = partial


def gate_back_kernel(
    grad_ref, y_ref, z_ref, stat_ref, out_weight_ref, gain_ref,
    dz_ref, dy_ref, scaled_ref, gain_grad_ref,
):
    @pl.when(pl.program_id(0) == 0)
    def _():
        gain_grad_ref[...] = jnp.zeros_like(gain_grad_ref)

    dscaled = dot(grad_ref[...], out_weight_ref[...])
    gate_z = z_ref[...]
    y = y_ref[...]
    gain = gain_ref[...]
    inv = stat_ref[:, 0:1]
    shift = stat_ref[:, 1:2] * inv * inv * inv * (1.0 / INNER)
    sig = jax.nn.sigmoid(gate_z)
    silu_z = gate_z * sig
    gated = y * silu_z
    normed = gated * inv
    scaled_ref[...] = (normed * gain).astype(LOW)
    gain_grad_ref[...] += jnp.sum(dscaled * normed, axis=0, keepdims=True)
    dgated = inv * gain * dscaled - gated * shift
    dz_ref[...] = (dgated * y * (sig + silu_z * (1.0 - sig))).astype(LOW)
    dy_ref[...] = dgated * silu_z


def scan_back_kernel(
    me_ref, dy_ref, y_ref, pre_ref, halo_ref, kept_ref, conv_ref, head_ref, skip_ref,
    spread_ref, gather_ref, dz_ref, z_weight_ref, weight_ref,
    grad_ref, dnormed_ref, conv_grad_ref, head_grad_ref, skip_grad_ref,
    dstate, ext, dext,
):
    size, width = dy_ref.shape
    conv_width = ext.shape[1]
    half = (conv_width - width) // 2
    step = pl.program_id(0)
    last_step = pl.num_programs(0) - 1

    @pl.when(step == 0)
    def _():
        dstate[...] = jnp.zeros_like(dstate)
        dext[size : size + 8, :] = jnp.zeros((8, conv_width), F32)
        conv_grad_ref[...] = jnp.zeros_like(conv_grad_ref)
        head_grad_ref[...] = jnp.zeros_like(head_grad_ref)
        skip_grad_ref[...] = jnp.zeros_like(skip_grad_ref)

    ext[0:8, :] = jnp.where(step == last_step, 0.0, halo_ref[:, :conv_width])
    ext[8 : 8 + size, :] = pre_ref[:, :conv_width]
    conv = conv_block(ext, conv_ref)
    sig = jax.nn.sigmoid(conv)
    act = conv * sig
    slope = sig + act * (1.0 - sig)
    inputs_x = act[:, :width]
    full_b = act[:, width : width + half]
    full_c = act[:, width + half :]
    low_b = full_b.astype(LOW)
    low_c = full_c.astype(LOW)
    left_b = left_parts(full_b, 1)
    pre_dt = pre_ref[:, conv_width:] + head_ref[0:1, :]
    step_dt = softplus(pre_dt)
    cum = decay_sums(step_dt, head_ref)
    cum_t = cum.T
    last = cum[size - 1 : size, :]
    spread = spread_ref[...]
    gather = gather_ref[...]
    dt_wide = dot(halves(step_dt), spread)
    cum_wide = dot(halves(jnp.exp2(cum)), spread)
    tail_wide = dot(halves(jnp.exp2(last - cum)), spread)
    scaled_x = inputs_x * dt_wide
    low_x = scaled_x.astype(LOW)
    tail_x = (scaled_x * tail_wide).astype(LOW)
    dy = dy_ref[...]
    high_dy, low_dy = split(dy)
    fade_dy = dy * cum_wide
    old_state = kept_ref[0]
    out_dstate = dstate[...]
    low_dstate = out_dstate.astype(LOW)
    tail_dx = tail_wide * dot(left_b, right_parts(out_dstate, 0))
    decay_all = cum_wide[size - 1 : size, :]
    state_sum = jnp.sum(old_state * out_dstate, axis=0, keepdims=True) * decay_all
    state_sum = state_sum + jnp.sum(scaled_x * tail_dx, axis=0, keepdims=True)
    state_dot = dot(halves(state_sum * jnp.ones((8, 1), F32)), gather)[0:1, :]
    dstate[...] = decay_all * out_dstate + dot(
        left_parts(full_c, 0), right_parts(fade_dy, 0), 0, 0
    )

    row = lax.broadcasted_iota(jnp.int32, (size, size), 0)
    col = lax.broadcasted_iota(jnp.int32, (size, size), 1)
    causal = col >= row
    affinity = jnp.where(causal, dot(left_b, right_parts(full_c, 1), 1, 1), 0.0)
    first_half = lax.broadcasted_iota(jnp.int32, (size, LANES), 1) < HEAD_WIDTH
    daffinity = jnp.zeros((size, size), F32)
    parts = []
    for pair in range(width // LANES):
        cols = slice(pair * LANES, (pair + 1) * LANES)
        pair_x = low_x[:, cols]
        pair_dy = high_dy[:, cols]
        both_dy = jnp.concatenate([pair_dy, low_dy[:, cols]], axis=1)
        zero = jnp.zeros_like(pair_x)
        here = []
        for which, head in enumerate((2 * pair, 2 * pair + 1)):
            gap = cum_t[head : head + 1, :] - cum[:, head : head + 1]
            fading = jnp.exp2(jnp.minimum(gap, 0.0))
            own_x = jnp.where(first_half, pair_x, zero) if which == 0 else jnp.where(first_half, zero, pair_x)
            daffinity = daffinity + fading * dot(own_x, pair_dy, 1, 1)
            here.append(mix_pair(affinity * fading, both_dy))
        parts.append(jnp.where(first_half, here[0], here[1]))
    low_daff = jnp.where(causal, daffinity, 0.0).astype(LOW)
    dx_wide = jnp.concatenate(parts, axis=1) + tail_dx
    d_b = dot(low_daff, low_c) + dot(tail_x, low_dstate, 1, 1)
    d_c = dot(low_daff, low_b, 0, 0) + dot(fade_dy.astype(LOW), old_state.astype(LOW), 1, 1)
    skip_x = skip_ref[0:1, :] * inputs_x
    from_y = dy * (y_ref[...] - skip_x) - scaled_x * dx_wide
    dcum = dot(halves(from_y), gather)
    from_dt = dot(halves(inputs_x * dx_wide), gather)
    upper = jnp.where(causal, 1.0, 0.0).astype(F32)
    da = dot(upper, dcum, precision=PRECISE) + state_dot
    ddt = from_dt + head_ref[2:3, :] * da
    dpre_dt = ddt * jax.nn.sigmoid(pre_dt)
    skip_grad_ref[0:1, :] += jnp.sum(dy * inputs_x, axis=0, keepdims=True)
    head_grad_ref[0:1, :] += jnp.sum(dpre_dt, axis=0, keepdims=True)
    head_grad_ref[1:2, :] += head_ref[2:3, :] * jnp.sum(step_dt * da, axis=0, keepdims=True)
    dinputs = dt_wide * dx_wide + skip_ref[0:1, :] * dy
    dconv = jnp.concatenate([dinputs, d_b, d_c], axis=1) * slope
    dext[0:size, :] = dconv
    inner = ext[8 : 8 + size, :]
    du = conv_ref[3:4, :] * dconv
    conv_grad_ref[4:5, :] += jnp.sum(dconv, axis=0, keepdims=True)
    conv_grad_ref[3:4, :] += jnp.sum(inner * dconv, axis=0, keepdims=True)
    for tap in range(3):
        moved = dext[3 - tap : 3 - tap + size, :]
        du = du + conv_ref[tap : tap + 1, :] * moved
        conv_grad_ref[tap : tap + 1, :] += jnp.sum(inner * moved, axis=0, keepdims=True)
    dext[size : size + 8, :] = dconv[0:8, :]
    low_grad = jnp.concatenate([du.astype(LOW), dpre_dt.astype(LOW)], axis=1)
    low_dz = dz_ref[...]
    grad_ref[:, :width] = low_dz
    grad_ref[:, width:] = low_grad
    dnormed = dot(low_dz, z_weight_ref[...], 1, 1) + dot(low_grad, weight_ref[...], 1, 1)
    dnormed_ref[...] = dnormed.astype(LOW)


def whole(shape):
    return pl.BlockSpec(shape, lambda *_: (0,) * len(shape))


def params():
    return pltpu.CompilerParams(
        vmem_limit_bytes=VMEM_BYTES, dimension_semantics=("arbitrary",)
    )


def spread_matrix(head_count, width):
    lanes = jnp.arange(LANES)[:, None]
    heads = (jnp.arange(width) // HEAD_WIDTH)[None, :]
    once = (lanes == heads).astype(LOW)
    return jnp.concatenate([once, once], axis=0)


def position(block, me, count, blocks_per_piece):
    slot = (block // blocks_per_piece) ^ me
    half = count // blocks_per_piece // 2
    return ((slot % 2) * half + slot // 2) * blocks_per_piece + block % blocks_per_piece


def scan_forward(me, rows, weight, conv_par, head_vals, skip, spread, blocks_per_piece, cover):
    total, depth = rows.shape
    width = skip.shape[1]
    conv_width = conv_par.shape[1]
    count = total // BLOCK
    pre_width = weight.shape[1]
    state_size = (conv_width - width) // 2

    def place(step, me_ref):
        return position(step, me_ref[0], count, blocks_per_piece)

    def at(step, me_ref):
        return (place(step, me_ref), 0)

    return pl.pallas_call(
        scan_kernel,
        out_shape=(
            jax.ShapeDtypeStruct((total, pre_width), F32),
            jax.ShapeDtypeStruct((total, width), F32),
            jax.ShapeDtypeStruct((count, state_size, width), F32),
        ),
        grid_spec=pltpu.PrefetchScalarGridSpec(
            num_scalar_prefetch=1,
            grid=(count,),
            in_specs=[
                pl.BlockSpec((BLOCK, depth), at),
                whole(weight.shape),
                whole(conv_par.shape),
                whole(head_vals.shape),
                whole(skip.shape),
                whole(spread.shape),
            ],
            out_specs=[
                pl.BlockSpec((BLOCK, pre_width), at),
                pl.BlockSpec((BLOCK, width), at),
                pl.BlockSpec((1, state_size, width), lambda step, me_ref: (step, 0, 0)),
            ],
            scratch_shapes=[
                pltpu.VMEM((state_size, width), F32),
                pltpu.VMEM((BLOCK + 8, conv_width), F32),
            ],
        ),
        compiler_params=params(),
        cost_estimate=pl.CostEstimate(
            flops=int(cover * total * depth * pre_width),
            bytes_accessed=total * width,
            transcendentals=0,
        ),
        name="scan_forward",
    )(me, rows, weight, conv_par, head_vals, skip, spread)


def gate_forward(rows, y, gate_weight, gain, z_all, part, blocks_per_piece):
    total, depth = rows.shape
    width = y.shape[1]
    count = total // BLOCK // blocks_per_piece
    middle = count // 2
    earlier = () if z_all is None else (z_all,)

    def spot(step):
        return (step + middle) % count

    def at(step):
        return (spot(step) * blocks_per_piece + part, 0)

    return pl.pallas_call(
        gate_kernel,
        out_shape=(
            jax.ShapeDtypeStruct((total, width), F32),
            jax.ShapeDtypeStruct((middle * BLOCK, depth), LOW),
            jax.ShapeDtypeStruct((middle * BLOCK, depth), LOW),
            jax.ShapeDtypeStruct((count * BLOCK, 1), F32),
        ),
        grid=(count,),
        in_specs=[
            pl.BlockSpec((BLOCK, depth), at),
            pl.BlockSpec((BLOCK, width), at),
            pl.BlockSpec((depth, width), lambda step: (0, 0)),
            pl.BlockSpec((depth, width), lambda step: (0, 1)),
            whole(gain.shape),
            *[pl.BlockSpec(memory_space=pl.ANY) for _ in earlier],
        ],
        out_specs=[
            pl.BlockSpec((BLOCK, width), at),
            pl.BlockSpec((BLOCK, depth), lambda step: (jnp.minimum(step, middle - 1), 0)),
            pl.BlockSpec((BLOCK, depth), lambda step: (jnp.maximum(step - middle, 0), 0)),
            pl.BlockSpec((BLOCK, 1), lambda step: (spot(step), 0)),
        ],
        input_output_aliases={5: 0} if earlier else {},
        compiler_params=params(),
        cost_estimate=pl.CostEstimate(
            flops=16 * count * BLOCK * depth * width,
            bytes_accessed=count * BLOCK * (4 * depth + 8 * width),
            transcendentals=count * BLOCK * width,
        ),
        name="gate_forward",
    )(rows, y, gate_weight, gate_weight, gain, *earlier)


def gate_backward(grad_rows, y, gate_z, stats, gate_weight, gain):
    total, depth = grad_rows.shape
    width = y.shape[1]

    def at(step):
        return (step, 0)

    return pl.pallas_call(
        gate_back_kernel,
        out_shape=(
            jax.ShapeDtypeStruct((total, width), LOW),
            jax.ShapeDtypeStruct((total, width), F32),
            jax.ShapeDtypeStruct((total, width), LOW),
            jax.ShapeDtypeStruct((1, width), F32),
        ),
        grid=(total // BLOCK,),
        in_specs=[
            pl.BlockSpec((BLOCK, depth), at),
            pl.BlockSpec((BLOCK, width), at),
            pl.BlockSpec((BLOCK, width), at),
            pl.BlockSpec((BLOCK, 2), at),
            pl.BlockSpec((depth, width), lambda step: (0, 1)),
            whole(gain.shape),
        ],
        out_specs=[
            pl.BlockSpec((BLOCK, width), at),
            pl.BlockSpec((BLOCK, width), at),
            pl.BlockSpec((BLOCK, width), at),
            whole(gain.shape),
        ],
        compiler_params=params(),
        cost_estimate=pl.CostEstimate(
            flops=total * width, bytes_accessed=total * width, transcendentals=0,
        ),
        name="gate_backward",
    )(grad_rows, y, gate_z, stats, gate_weight, gain)


def scan_backward(
    me, dy, y, pre, kept, conv_par, head_vals, skip, spread, dz, gate_weight, weight, blocks_per_piece
):
    total, width = dy.shape
    pre_width = pre.shape[1]
    conv_width = conv_par.shape[1]
    state_size = kept.shape[1]
    count = total // BLOCK
    halo_blocks = BLOCK // 8
    gather = spread.T
    gather = jnp.concatenate([gather[:, :LANES]] * 2, axis=0)

    def place(block, me_ref):
        return position(block, me_ref[0], count, blocks_per_piece)

    def at(step, me_ref):
        return (place(count - 1 - step, me_ref), 0)

    def parted(step, me_ref):
        spot = place(count - 1 - step, me_ref)
        return ((spot % blocks_per_piece) * (count // blocks_per_piece) + spot // blocks_per_piece, 0)

    def before(step, me_ref):
        return (place(jnp.maximum(count - 2 - step, 0), me_ref) * halo_blocks + halo_blocks - 1, 0)

    return pl.pallas_call(
        scan_back_kernel,
        out_shape=(
            jax.ShapeDtypeStruct((total, width + pre_width), LOW),
            jax.ShapeDtypeStruct((total, weight.shape[0]), LOW),
            jax.ShapeDtypeStruct((8, conv_width), F32),
            jax.ShapeDtypeStruct((8, LANES), F32),
            jax.ShapeDtypeStruct((8, width), F32),
        ),
        grid_spec=pltpu.PrefetchScalarGridSpec(
            num_scalar_prefetch=1,
            grid=(count,),
            in_specs=[
                pl.BlockSpec((BLOCK, width), at),
                pl.BlockSpec((BLOCK, width), at),
                pl.BlockSpec((BLOCK, pre_width), at),
                pl.BlockSpec((8, pre_width), before),
                pl.BlockSpec((1, state_size, width), lambda step, me_ref: (count - 1 - step, 0, 0)),
                whole(conv_par.shape),
                whole(head_vals.shape),
                whole(skip.shape),
                whole(spread.shape),
                whole(gather.shape),
                pl.BlockSpec((BLOCK, width), at),
                pl.BlockSpec((weight.shape[0], width), lambda step, me_ref: (0, 0)),
                whole(weight.shape),
            ],
            out_specs=[
                pl.BlockSpec((BLOCK, width + pre_width), at),
                pl.BlockSpec((BLOCK, weight.shape[0]), parted),
                whole((8, conv_width)),
                whole((8, LANES)),
                whole((8, width)),
            ],
            scratch_shapes=[
                pltpu.VMEM((state_size, width), F32),
                pltpu.VMEM((BLOCK + 8, conv_width), F32),
                pltpu.VMEM((BLOCK + 8, conv_width), F32),
            ],
        ),
        compiler_params=params(),
        cost_estimate=pl.CostEstimate(
            flops=total * width, bytes_accessed=total * width, transcendentals=0,
        ),
        name="scan_backward",
    )(me, dy, y, pre, pre, kept, conv_par, head_vals, skip, spread, gather, dz, gate_weight, weight)


def root_kernel(rows_ref, root_ref):
    vals = rows_ref[...]
    root_ref[...] = lax.rsqrt(jnp.mean(vals * vals, axis=1, keepdims=True) + NORM_EPS)


def first_root(rows):
    return pl.pallas_call(
        root_kernel,
        out_shape=jax.ShapeDtypeStruct((rows.shape[0], 1), F32),
        compiler_params=pltpu.CompilerParams(vmem_limit_bytes=VMEM_BYTES),
        cost_estimate=pl.CostEstimate(flops=10**11, bytes_accessed=rows.size * 4, transcendentals=0),
        name="first_root",
    )(rows)


def swap(vals, distance, count):
    return lax.ppermute(vals, "tensor", [(src, src ^ distance) for src in range(count)])


def gather_pieces(own, count):
    far = swap(own, 2, count)
    return [own, far, swap(own, 1, count), swap(far, 1, count)]


def gather_slots(own, count, beside=None):
    far = swap(own, 2, count)
    if beside is not None:
        far, beside = lax.optimization_barrier((far, beside))
    full = jnp.concatenate([own, far, swap(own, 1, count), swap(far, 1, count)], axis=0)
    return full if beside is None else (full, beside)


def gather_parts(parts, kept, count):
    parts = list(parts)
    gathered = []
    for spot, part in enumerate(parts):
        far = swap(part, 2, count)
        if spot + 1 < len(parts):
            far, parts[spot + 1] = lax.optimization_barrier((far, parts[spot + 1]))
        gathered.append([kept[spot], far, swap(part, 1, count), swap(far, 1, count)])
    return jnp.concatenate([part[spot] for spot in range(count) for part in gathered], axis=0)


def reduce_slots(sent, held, count, wire):
    return reduce_far(reduce_near(sent, held, count, wire), count, wire)


def reduce_near(sent, held, count, wire):
    return held.astype(F32) + swap(sent.astype(wire), 1, count).astype(F32)


def reduce_far(near, count, wire):
    return add_far(near, swap_far(near, count, wire))


def swap_far(near, count, wire):
    return swap(near[near.shape[0] // 2 :].astype(wire), 2, count)


def add_far(near, far):
    return near[: far.shape[0]] + far.astype(F32)


def ring_index(place, count):
    return jnp.where(place < count // 2, 2 * place, 2 * (count - place) - 1)


def ring_place(index, count):
    return jnp.where(index % 2 == 0, index // 2, count - (index + 1) // 2)


def ring_step(vals, way, count):
    order = list(range(0, count, 2)) + list(range(count - 1, 0, -2))
    pairs = [(order[spot], order[(spot + way) % count]) for spot in range(count)]
    return lax.ppermute(vals, "dp", pairs)


class RingReduce:
    def __init__(self, vals, count):
        self.vals, self.count = vals, count
        self.share = vals.shape[0] // count
        self.place = ring_place(lax.axis_index("dp"), count)
        self.total_hops = count // 2
        self.hops = {1: count // 2, -1: count - 1 - count // 2}
        self.moving = {way: self.chunk(way * hops).astype(LOW) for way, hops in self.hops.items()}
        self.done = 0

    def chunk(self, offset):
        index = ring_index((self.place + offset) % self.count, self.count)
        return lax.dynamic_slice_in_dim(self.vals, index * self.share, self.share, 0).astype(F32)

    def hop(self):
        self.done += 1
        for way, hops in self.hops.items():
            if self.done > hops:
                continue
            moved = ring_step(self.moving[way], way, self.count)
            if self.done < hops:
                moved = (moved.astype(F32) + self.chunk(way * (hops - self.done))).astype(LOW)
            self.moving[way] = moved

    def finish(self):
        while self.done < self.total_hops:
            self.hop()
        return self.chunk(0) + self.moving[1].astype(F32) + self.moving[-1].astype(F32)


def xor_step(vals, axis, distance, count):
    return lax.ppermute(vals, axis, [(src, src ^ distance) for src in range(count)])


def xor_sum(vals, axis, count):
    distance = 1
    while distance < count:
        vals = vals + xor_step(vals, axis, distance, count)
        distance *= 2
    return vals


def xor_gather(own, dp_count, tensor_count):
    stack = own
    for axis, count in (("dp", dp_count), ("tensor", tensor_count)):
        distance = 1
        while distance < count:
            stack = jnp.concatenate([stack, xor_step(stack, axis, distance, count)], axis=0)
            distance *= 2
    total = dp_count * tensor_count
    spots = jnp.arange(total)
    owner = (lax.axis_index("dp") ^ (spots % dp_count)) * tensor_count + (
        lax.axis_index("tensor") ^ (spots // dp_count)
    )
    chosen = owner[None, :] == spots[:, None]
    return jnp.sum(jnp.where(chosen[:, :, None], stack[None], 0.0), axis=1)


def adam_update(current, gradient, moment_old, square_old, step_rate, decay_coef):
    moment_new = BETA_ONE * moment_old + (1.0 - BETA_ONE) * gradient
    square_new = BETA_TWO * square_old + (1.0 - BETA_TWO) * gradient * gradient
    moment_hat = moment_new / (1.0 - BETA_ONE**STEP)
    square_hat = square_new / (1.0 - BETA_TWO**STEP)
    updated = current - step_rate * (
        moment_hat / (jnp.sqrt(square_hat) + ADAM_EPS) + decay_coef * current
    )
    return (updated, moment_new, square_new)


def inv_rms(vals):
    return lax.rsqrt(jnp.mean(vals * vals, axis=1, keepdims=True) + NORM_EPS)


def pad_rows(vals, rows):
    return jnp.pad(vals, ((0, rows - vals.shape[0]), (0, 0)))


def pad_lanes(vals, lanes):
    return jnp.pad(vals, ((0, 0), (0, lanes - vals.shape[1])))


def local(
    dp_count,
    tensor_count,
    resid_in,
    cotangent,
    w_zx,
    w_bc,
    w_dt,
    w_out,
    chan_par,
    head_par,
    bc_par,
    norm_gain,
    zx_first,
    zx_second,
    bc_first,
    bc_second,
    dt_first,
    dt_second,
    out_first,
    out_second,
    chan_first,
    chan_second,
    head_first,
    head_second,
    bcpar_first,
    bcpar_second,
    gain_first,
    gain_second,
):
    layer_total, depth_share, _, width = w_zx.shape
    rows_own, depth = resid_in.shape
    head_count = w_dt.shape[2]
    state_two = w_bc.shape[2]
    conv_width = width + state_two
    tap_total = bc_par.shape[1]
    pieces = rows_own // BLOCK
    me_dp = lax.axis_index("dp")
    me_tensor = lax.axis_index("tensor")
    me = me_tensor.astype(jnp.int32).reshape((1,))
    place = me_dp * tensor_count + me_tensor

    gain_share, bcpar_share = norm_gain.shape[1], bc_par.shape[2]
    flat = jnp.concatenate([norm_gain.reshape(-1), bc_par.reshape(-1)])[None, :]
    bc_weights = lax.all_gather(w_bc.astype(LOW), "tensor", axis=1, tiled=True)
    bc_weights, opening = lax.optimization_barrier((bc_weights, resid_in))
    flat, opening = lax.optimization_barrier((flat, first_root(opening)))
    weights = []
    for layer in range(layer_total):
        scan_share = jnp.concatenate(
            [
                w_zx[layer, :, 1, :].astype(LOW),
                bc_weights[layer],
                pad_lanes(w_dt[layer].astype(LOW), LANES),
            ],
            axis=1,
        )
        gate_share = jnp.concatenate(
            [w_zx[layer, :, 0, :].astype(LOW), w_out[layer].T.astype(LOW)], axis=1
        )
        if layer == 0:
            small = xor_gather(flat, dp_count, tensor_count)
        scan_weight = lax.all_gather(scan_share, "dp", axis=0, tiled=True)
        gate_weight = lax.all_gather(gate_share, "dp", axis=0, tiled=True)
        weights.append((scan_weight, gate_weight))
    gain_len = layer_total * gain_share
    gain_all = small[:, :gain_len].reshape(-1, layer_total, gain_share)
    gain_all = gain_all.transpose(1, 0, 2).reshape(layer_total, depth)
    bcpar_all = small[:, gain_len:].reshape(-1, layer_total, tap_total, bcpar_share)
    bcpar_all = bcpar_all.transpose(1, 2, 0, 3).reshape(layer_total, tap_total, state_two)

    spread = spread_matrix(head_count, width)
    def in_parts(vals):
        return [vals[part * BLOCK : (part + 1) * BLOCK] for part in range(pieces)]

    def in_turn(far_list, make):
        made, ready = [], []
        for spot, far in enumerate(far_list):
            if spot:
                far, held = lax.optimization_barrier((far, made[-1][0]))
                ready.append(held)
            made.append(make(spot, far))
        ready.append(made[-1][0])
        return made, ready

    hidden = in_parts(resid_in)
    roots = in_parts(opening)
    low_rows = ready_rows = None
    kept = []
    for layer in range(layer_total):
        scan_weight, gate_weight = weights[layer]
        conv_par = pad_rows(jnp.concatenate([chan_par[layer, :-1], bcpar_all[layer]], axis=1), 8)
        decay = -jnp.exp(head_par[layer, 1])
        head_vals = pad_rows(
            pad_lanes(jnp.stack([head_par[layer, 0], decay * LOG2E, decay], 0), LANES), 8
        )
        skip = pad_rows(jnp.repeat(head_par[layer, 2], HEAD_WIDTH)[None, :], 8)
        gain_q = chan_par[layer, -1:]
        if layer == 0:
            normed = (resid_in * opening * gain_all[layer][None, :]).astype(LOW)
            rows, scan_weight = gather_slots(normed, tensor_count, scan_weight)
            weights[0] = (scan_weight, gate_weight)
            rows, first_grad = lax.optimization_barrier((rows, cotangent.astype(LOW)))
            first_far = swap(first_grad, 2, tensor_count)
        else:
            rows = gather_parts(low_rows, ready_rows, tensor_count)
        pre, y, states = scan_forward(
            me, rows, scan_weight, conv_par, head_vals, skip, spread, pieces, 0.1 if layer else 8.0
        )
        if layer == 0:
            y, first_far = lax.optimization_barrier((y, first_far))
            first_full = jnp.concatenate(
                [first_grad, first_far, swap(first_grad, 1, tensor_count), swap(first_far, 1, tensor_count)], axis=0
            )
        gate_z = None
        far_list, near_list, inv_list = [], [], []
        for part in range(pieces):
            gate_z, sent, held, squares = gate_forward(rows, y, gate_weight, gain_q, gate_z, part, pieces)
            near = reduce_near(sent, held, tensor_count, LOW)
            near, squares = lax.optimization_barrier((near, squares))
            middle = squares.shape[0] // 2
            square_own = reduce_slots(squares[middle:], squares[:middle], tensor_count, F32)
            inv_list.append(lax.rsqrt(square_own / INNER + NORM_EPS))
            near_list.append(near)
            far_list.append(swap_far(near, tensor_count, LOW))
        next_gain = gain_all[min(layer + 1, layer_total - 1)][None, :]

        def next_rows(spot, far, near_list=near_list, inv_list=inv_list, hidden=hidden, next_gain=next_gain):
            branch = add_far(near_list[spot], far)
            out = hidden[spot] + inv_list[spot] * branch
            root = inv_rms(out)
            return (out * root * next_gain).astype(LOW), out, root, branch

        made, ready_rows = in_turn(far_list, next_rows)
        kept.append(
            (
                hidden, roots, rows, pre, y, states, gate_z, inv_list, [entry[3] for entry in made],
                conv_par, head_vals, skip, gain_q,
            )
        )
        low_rows = [entry[0] for entry in made]
        hidden = [entry[1] for entry in made]
        roots = [entry[2] for entry in made]

    grad_hidden = in_parts(cotangent)
    zx_list = [None] * layer_total
    dt_list = [None] * layer_total
    out_list = [None] * layer_total
    bc_list = [None] * layer_total
    small_list = [None] * layer_total
    shared_list = [None] * layer_total
    gain_list = [None] * layer_total
    def place_scan(layer, total):
        z_sum, scan_sum = total[:, :width], total[:, width:]
        zx_list[layer] = jnp.stack([z_sum, scan_sum[:, :width]], axis=1)
        share = depth_share // tensor_count
        parts = [
            lax.dynamic_slice_in_dim(scan_sum[:, width:conv_width], (me_tensor ^ slot) * share, share, 0)
            for slot in [*range(0, tensor_count, 2), *range(1, tensor_count, 2)]
        ]
        middle = tensor_count // 2
        bc_list[layer] = reduce_slots(
            jnp.concatenate(parts[middle:], axis=0), jnp.concatenate(parts[:middle], axis=0), tensor_count, F32
        )
        dt_list[layer] = scan_sum[:, conv_width : conv_width + head_count]

    late = ()

    def owned(grad):
        return lax.psum_scatter(grad, "dp", scatter_dimension=0, tiled=True)

    for layer in reversed(range(layer_total)):
        scan_weight, gate_weight = weights[layer]
        (
            entering, roots, rows, pre, y, states, gate_z, inv_list, projected, conv_par, head_vals, skip, gain_q,
        ) = kept[layer]
        if layer == layer_total - 1:
            branch_low = [part.astype(LOW) for part in grad_hidden]
        stats = [
            jnp.concatenate([inv, jnp.sum(low.astype(F32) * branch, axis=1, keepdims=True)], axis=1)
            for inv, low, branch in zip(inv_list, branch_low, projected)
        ]
        stats = gather_slots(jnp.concatenate(stats, axis=0), tensor_count)
        full_grad = first_full if layer == layer_total - 1 else gather_parts(branch_low, ready_low, tensor_count)
        dz, dy, scaled, gain_five = gate_backward(full_grad, y, gate_z, stats, gate_weight, gain_q)
        out_grad = dot(full_grad, scaled, 0, 0).astype(LOW)
        dy, out_grad = lax.optimization_barrier((dy, out_grad))
        if layer + 1 < layer_total:
            late, out_grad = lax.optimization_barrier((late, out_grad))
            place_scan(layer + 1, late.astype(F32))
        out_sum = owned(out_grad)
        dmerged, dnormed, conv_grad, head_grad, skip_grad = scan_backward(
            me, dy, y, pre, states, conv_par, head_vals, skip, spread, dz, gate_weight, scan_weight, pieces
        )
        out_sum, dnormed, dmerged = lax.optimization_barrier((out_sum, dnormed, dmerged))
        part_rows = dnormed.shape[0] // pieces
        near_list = []
        for part in range(pieces):
            vals = dnormed[part * part_rows : (part + 1) * part_rows]
            near_list.append(
                reduce_near(vals[part_rows // 2 :], vals[: part_rows // 2], tensor_count, LOW)
            )
        merged_grad = dot(rows, dmerged, 0, 0)
        if layer == 0:
            small_sums = (conv_grad, head_grad, skip_grad, gain_five)
            near_list, merged_grad, small_sums = lax.optimization_barrier((near_list, merged_grad, small_sums))
            conv_grad, head_grad, skip_grad, gain_five = small_sums
        far_list = [swap_far(near, tensor_count, LOW) for near in near_list]
        if layer == 0:
            place_scan(layer, RingReduce(merged_grad, dp_count).finish())
        else:
            far_list[-1], merged_grad = lax.optimization_barrier((far_list[-1], merged_grad.astype(LOW)))
            late = owned(merged_grad)
        out_list[layer] = out_sum.astype(F32).T
        gain = gain_all[layer][None, :]

        def next_grad(
            spot, far, near_list=near_list, entering=entering, roots=roots, grad_hidden=grad_hidden, gain=gain
        ):
            part_grad = add_far(near_list[spot], far)
            part_in, root = entering[spot], roots[spot]
            gained = part_grad * gain
            shift = jnp.mean(gained * part_in, axis=1, keepdims=True) * root * root * root
            out = grad_hidden[spot] + root * gained - part_in * shift
            return out.astype(LOW), out, jnp.sum(part_grad * part_in * root, axis=0)

        made, ready_low = in_turn(far_list, next_grad)
        branch_low = [entry[0] for entry in made]
        grad_hidden = [entry[1] for entry in made]
        gain_grad = sum(entry[2] for entry in made)

        chan_grad = jnp.concatenate([conv_grad[:5, :width], gain_five], axis=0)
        skip_sum = skip_grad[0].reshape(head_count, HEAD_WIDTH).sum(axis=1)
        head_all = jnp.concatenate(
            [head_grad[0, :head_count], head_grad[1, :head_count], skip_sum]
        )
        small_list[layer] = jnp.concatenate([chan_grad.reshape(-1), head_all])
        gain_list[layer] = gain_grad
        shared_list[layer] = conv_grad[:5, width:].reshape(-1)

    shared = xor_sum(jnp.stack(shared_list, 0), "tensor", tensor_count)
    both = xor_sum(jnp.concatenate([jnp.stack(small_list, 0), shared], axis=1), "dp", dp_count)
    chan_len = chan_par.shape[1] * width
    head_len = head_par.shape[1] * head_count
    chan_stack = both[:, :chan_len].reshape(chan_par.shape)
    head_stack = both[:, chan_len : chan_len + head_len].reshape(head_par.shape)
    shared = both[:, chan_len + head_len :]
    gains = xor_sum(xor_sum(jnp.stack(gain_list, 0), "tensor", tensor_count), "dp", dp_count)
    gain_stack = lax.dynamic_slice_in_dim(gains, place * gain_share, gain_share, axis=1)
    bcpar_stack = lax.dynamic_slice_in_dim(
        shared.reshape(layer_total, tap_total, state_two), place * bcpar_share, bcpar_share, axis=2
    )

    zx_stack = with_layout_constraint(jnp.stack(zx_list, 0), Layout((0, 1, 2, 3)))
    zx_new = adam_update(w_zx, zx_stack, zx_first, zx_second, MATRIX_RATE, MATRIX_DECAY)
    bc_new = adam_update(w_bc, jnp.stack(bc_list, 0), bc_first, bc_second, MATRIX_RATE, MATRIX_DECAY)
    dt_new = adam_update(w_dt, jnp.stack(dt_list, 0), dt_first, dt_second, MATRIX_RATE, MATRIX_DECAY)
    out_new = adam_update(w_out, jnp.stack(out_list, 0), out_first, out_second, MATRIX_RATE, MATRIX_DECAY)
    chan_new = adam_update(chan_par, chan_stack, chan_first, chan_second, SMALL_RATE, 0.0)
    head_new = adam_update(head_par, head_stack, head_first, head_second, HEAD_RATE, 0.0)
    bcpar_new = adam_update(bc_par, bcpar_stack, bcpar_first, bcpar_second, SMALL_RATE, 0.0)
    gain_new = adam_update(norm_gain, gain_stack, gain_first, gain_second, SMALL_RATE, 0.0)
    return (
        jnp.concatenate(hidden, axis=0), jnp.concatenate(grad_hidden, axis=0), *zx_new, *bc_new, *dt_new, *out_new, *chan_new, *head_new, *bcpar_new, *gain_new,
    )


def solution(mesh):
    in_specs = (
        P(("dp", "tensor"), None),
        P(("dp", "tensor"), None),
        P(None, "dp", None, "tensor"),
        P(None, ("dp", "tensor"), None),
        P(None, "dp", "tensor"),
        P(None, "tensor", "dp"),
        P(None, None, "tensor"),
        P(None, None, "tensor"),
        P(None, None, ("dp", "tensor")),
        P(None, ("dp", "tensor")),
        P(None, "dp", None, "tensor"),
        P(None, "dp", None, "tensor"),
        P(None, ("dp", "tensor"), None),
        P(None, ("dp", "tensor"), None),
        P(None, "dp", "tensor"),
        P(None, "dp", "tensor"),
        P(None, "tensor", "dp"),
        P(None, "tensor", "dp"),
        P(None, None, "tensor"),
        P(None, None, "tensor"),
        P(None, None, "tensor"),
        P(None, None, "tensor"),
        P(None, None, ("dp", "tensor")),
        P(None, None, ("dp", "tensor")),
        P(None, ("dp", "tensor")),
        P(None, ("dp", "tensor")),
    )
    out_specs = (
        P(("dp", "tensor"), None),
        P(("dp", "tensor"), None),
        P(None, "dp", None, "tensor"),
        P(None, "dp", None, "tensor"),
        P(None, "dp", None, "tensor"),
        P(None, ("dp", "tensor"), None),
        P(None, ("dp", "tensor"), None),
        P(None, ("dp", "tensor"), None),
        P(None, "dp", "tensor"),
        P(None, "dp", "tensor"),
        P(None, "dp", "tensor"),
        P(None, "tensor", "dp"),
        P(None, "tensor", "dp"),
        P(None, "tensor", "dp"),
        P(None, None, "tensor"),
        P(None, None, "tensor"),
        P(None, None, "tensor"),
        P(None, None, "tensor"),
        P(None, None, "tensor"),
        P(None, None, "tensor"),
        P(None, None, ("dp", "tensor")),
        P(None, None, ("dp", "tensor")),
        P(None, None, ("dp", "tensor")),
        P(None, ("dp", "tensor")),
        P(None, ("dp", "tensor")),
        P(None, ("dp", "tensor")),
    )
    return jax.shard_map(
        functools.partial(local, mesh.shape["dp"], mesh.shape["tensor"]), mesh=mesh, in_specs=in_specs, out_specs=out_specs, check_vma=False)
```

```python
import functools
import math

import jax
import jax.numpy as jnp
from jax import lax
from jax.experimental import pallas as pl
from jax.experimental.layout import Layout, with_layout_constraint
from jax.experimental.pallas import tpu as pltpu
from jax.sharding import PartitionSpec as P

BLOCK = 256
STEP = 10
INNER = 3072
LANES = 128
HEAD_WIDTH = 64

NORM_EPS = 1e-05
BETA_ONE = 0.9
BETA_TWO = 0.95
ADAM_EPS = 1e-08
MATRIX_RATE = 0.02
MATRIX_DECAY = 0.1
SMALL_RATE = 0.3
HEAD_RATE = 2.0
PRECISE = lax.Precision.HIGHEST
LOG2E = math.log2(math.e)
LOW = jnp.bfloat16
F32 = jnp.float32
VMEM_BYTES = 56 * 1024 * 1024


def dot(left, right, left_dim=1, right_dim=0, precision=None):
    return lax.dot_general(
        left,
        right,
        (((left_dim,), (right_dim,)), ((), ())),
        preferred_element_type=F32,
        precision=precision,
    )


def split(vals):
    high = vals.astype(LOW)
    return high, (vals - high.astype(F32)).astype(LOW)


def halves(vals):
    return jnp.concatenate(split(vals), axis=1)


def left_parts(vals, axis):
    high, low = split(vals)
    return jnp.concatenate([high, low, high], axis=axis)


def right_parts(vals, axis):
    high, low = split(vals)
    return jnp.concatenate([high, high, low], axis=axis)


def mix_pair(mixing, pair):
    out = dot(jnp.concatenate(split(mixing), axis=1), jnp.concatenate([pair, pair], axis=0))
    return out[:, :LANES] + out[:, LANES:]


def softplus(vals):
    return jnp.maximum(vals, 0.0) + jnp.log1p(jnp.exp(-jnp.abs(vals)))


def conv_block(ext, conv_ref):
    rows = ext.shape[0] - 8
    total = conv_ref[4:5, :] + conv_ref[3:4, :] * ext[8 : 8 + rows, :]
    for tap in range(3):
        total = total + conv_ref[tap : tap + 1, :] * ext[5 + tap : 5 + tap + rows, :]
    return total


def decay_sums(step_dt, head_ref):
    size = step_dt.shape[0]
    row = lax.broadcasted_iota(jnp.int32, (size, size), 0)
    col = lax.broadcasted_iota(jnp.int32, (size, size), 1)
    lower = jnp.where(row >= col, 1.0, 0.0).astype(F32)
    return dot(lower, step_dt * head_ref[1:2, :], precision=PRECISE)


def scan_kernel(
    me_ref, rows_ref, weight_ref, conv_ref, head_ref, skip_ref, spread_ref,
    pre_ref, y_ref, kept_ref, state, ext,
):
    width = y_ref.shape[1]
    conv_width = ext.shape[1]
    half = (conv_width - width) // 2
    size = rows_ref.shape[0]

    @pl.when(pl.program_id(0) == 0)
    def _():
        state[...] = jnp.zeros_like(state)
        ext[0:8, :] = jnp.zeros((8, conv_width), F32)

    @pl.when(pl.program_id(0) > 0)
    def _():
        ext[0:8, :] = ext[size : size + 8, :]

    pre = dot(rows_ref[...], weight_ref[...])
    pre_ref[...] = pre
    ext[8 : 8 + size, :] = pre[:, :conv_width]
    conv = conv_block(ext, conv_ref)
    act = conv * jax.nn.sigmoid(conv)
    inputs_x = act[:, :width]
    left_c = left_parts(act[:, width + half :], 1)
    step_dt = softplus(pre[:, conv_width:] + head_ref[0:1, :])
    cum = decay_sums(step_dt, head_ref)
    cum_t = cum.T
    last = cum[size - 1 : size, :]
    spread = spread_ref[...]
    dt_wide = dot(halves(step_dt), spread)
    cum_wide = dot(halves(jnp.exp2(cum)), spread)
    tail_wide = dot(halves(jnp.exp2(last - cum)), spread)
    scaled_x = inputs_x * dt_wide
    high_x, low_x = split(scaled_x)
    row = lax.broadcasted_iota(jnp.int32, (size, size), 0)
    col = lax.broadcasted_iota(jnp.int32, (size, size), 1)
    affinity = jnp.where(row >= col, dot(left_c, right_parts(act[:, width : width + half], 1), 1, 1), 0.0)
    old_state = state[...]
    kept_ref[0] = old_state
    y_ref[...] = (
        cum_wide * dot(left_c, right_parts(old_state, 0)) + skip_ref[0:1, :] * inputs_x
    )
    state[...] = cum_wide[size - 1 : size, :] * old_state + dot(
        left_parts(act[:, width : width + half], 0), right_parts(scaled_x * tail_wide, 0), 0, 0
    )
    first_half = lax.broadcasted_iota(jnp.int32, (size, LANES), 1) < HEAD_WIDTH
    for pair in range(width // LANES):
        cols = slice(pair * LANES, (pair + 1) * LANES)
        pair_x = jnp.concatenate([high_x[:, cols], low_x[:, cols]], axis=1)
        parts = []
        for head in (2 * pair, 2 * pair + 1):
            gap = cum[:, head : head + 1] - cum_t[head : head + 1, :]
            parts.append(mix_pair(affinity * jnp.exp2(jnp.minimum(gap, 0.0)), pair_x))
        y_ref[:, cols] += jnp.where(first_half, parts[0], parts[1])


def gate_kernel(rows_ref, y_ref, z_weight_ref, out_weight_ref, gain_ref, *refs):
    z_ref, sent_ref, own_ref, sq_ref = refs[-4:]
    gate_z = dot(rows_ref[...], z_weight_ref[...])
    z_ref[...] = gate_z
    gated = y_ref[...] * (gate_z * jax.nn.sigmoid(gate_z))
    sq_ref[...] = jnp.sum(gated * gated, axis=1, keepdims=True)
    low_gated = (gated * gain_ref[...]).astype(LOW)
    partial = dot(low_gated, out_weight_ref[...], 1, 1).astype(LOW)
    sending = pl.program_id(0) < pl.num_programs(0) // 2

    @pl.when(sending)
    def _():
        sent_ref[...] = partial

    @pl.when(jnp.logical_not(sending))
    def _():
        own_ref[...] = partial


def gate_back_kernel(
    grad_ref, y_ref, z_ref, stat_ref, out_weight_ref, gain_ref,
    dz_ref, dy_ref, scaled_ref, gain_grad_ref,
):
    @pl.when(pl.program_id(0) == 0)
    def _():
        gain_grad_ref[...] = jnp.zeros_like(gain_grad_ref)

    dscaled = dot(grad_ref[...], out_weight_ref[...])
    gate_z = z_ref[...]
    y = y_ref[...]
    gain = gain_ref[...]
    inv = stat_ref[:, 0:1]
    shift = stat_ref[:, 1:2] * inv * inv * inv * (1.0 / INNER)
    sig = jax.nn.sigmoid(gate_z)
    silu_z = gate_z * sig
    gated = y * silu_z
    normed = gated * inv
    scaled_ref[...] = (normed * gain).astype(LOW)
    gain_grad_ref[...] += jnp.sum(dscaled * normed, axis=0, keepdims=True)
    dgated = inv * gain * dscaled - gated * shift
    dz_ref[...] = (dgated * y * (sig + silu_z * (1.0 - sig))).astype(LOW)
    dy_ref[...] = dgated * silu_z


def scan_back_kernel(
    me_ref, dy_ref, y_ref, pre_ref, halo_ref, kept_ref, conv_ref, head_ref, skip_ref,
    spread_ref, gather_ref, dz_ref, z_weight_ref, weight_ref,
    grad_ref, dnormed_ref, conv_grad_ref, head_grad_ref, skip_grad_ref,
    dstate, ext, dext,
):
    size, width = dy_ref.shape
    conv_width = ext.shape[1]
    half = (conv_width - width) // 2
    step = pl.program_id(0)
    last_step = pl.num_programs(0) - 1

    @pl.when(step == 0)
    def _():
        dstate[...] = jnp.zeros_like(dstate)
        dext[size : size + 8, :] = jnp.zeros((8, conv_width), F32)
        conv_grad_ref[...] = jnp.zeros_like(conv_grad_ref)
        head_grad_ref[...] = jnp.zeros_like(head_grad_ref)
        skip_grad_ref[...] = jnp.zeros_like(skip_grad_ref)

    ext[0:8, :] = jnp.where(step == last_step, 0.0, halo_ref[:, :conv_width])
    ext[8 : 8 + size, :] = pre_ref[:, :conv_width]
    conv = conv_block(ext, conv_ref)
    sig = jax.nn.sigmoid(conv)
    act = conv * sig
    slope = sig + act * (1.0 - sig)
    inputs_x = act[:, :width]
    full_b = act[:, width : width + half]
    full_c = act[:, width + half :]
    low_b = full_b.astype(LOW)
    low_c = full_c.astype(LOW)
    left_b = left_parts(full_b, 1)
    pre_dt = pre_ref[:, conv_width:] + head_ref[0:1, :]
    step_dt = softplus(pre_dt)
    cum = decay_sums(step_dt, head_ref)
    cum_t = cum.T
    last = cum[size - 1 : size, :]
    spread = spread_ref[...]
    gather = gather_ref[...]
    dt_wide = dot(halves(step_dt), spread)
    cum_wide = dot(halves(jnp.exp2(cum)), spread)
    tail_wide = dot(halves(jnp.exp2(last - cum)), spread)
    scaled_x = inputs_x * dt_wide
    low_x = scaled_x.astype(LOW)
    tail_x = (scaled_x * tail_wide).astype(LOW)
    dy = dy_ref[...]
    high_dy, low_dy = split(dy)
    fade_dy = dy * cum_wide
    old_state = kept_ref[0]
    out_dstate = dstate[...]
    low_dstate = out_dstate.astype(LOW)
    tail_dx = tail_wide * dot(left_b, right_parts(out_dstate, 0))
    decay_all = cum_wide[size - 1 : size, :]
    state_sum = jnp.sum(old_state * out_dstate, axis=0, keepdims=True) * decay_all
    state_sum = state_sum + jnp.sum(scaled_x * tail_dx, axis=0, keepdims=True)
    state_dot = dot(halves(state_sum * jnp.ones((8, 1), F32)), gather)[0:1, :]
    dstate[...] = decay_all * out_dstate + dot(
        left_parts(full_c, 0), right_parts(fade_dy, 0), 0, 0
    )

    row = lax.broadcasted_iota(jnp.int32, (size, size), 0)
    col = lax.broadcasted_iota(jnp.int32, (size, size), 1)
    causal = col >= row
    affinity = jnp.where(causal, dot(left_b, right_parts(full_c, 1), 1, 1), 0.0)
    first_half = lax.broadcasted_iota(jnp.int32, (size, LANES), 1) < HEAD_WIDTH
    daffinity = jnp.zeros((size, size), F32)
    parts = []
    for pair in range(width // LANES):
        cols = slice(pair * LANES, (pair + 1) * LANES)
        pair_x = low_x[:, cols]
        pair_dy = high_dy[:, cols]
        both_dy = jnp.concatenate([pair_dy, low_dy[:, cols]], axis=1)
        zero = jnp.zeros_like(pair_x)
        here = []
        for which, head in enumerate((2 * pair, 2 * pair + 1)):
            gap = cum_t[head : head + 1, :] - cum[:, head : head + 1]
            fading = jnp.exp2(jnp.minimum(gap, 0.0))
            own_x = jnp.where(first_half, pair_x, zero) if which == 0 else jnp.where(first_half, zero, pair_x)
            daffinity = daffinity + fading * dot(own_x, pair_dy, 1, 1)
            here.append(mix_pair(affinity * fading, both_dy))
        parts.append(jnp.where(first_half, here[0], here[1]))
    low_daff = jnp.where(causal, daffinity, 0.0).astype(LOW)
    dx_wide = jnp.concatenate(parts, axis=1) + tail_dx
    d_b = dot(low_daff, low_c) + dot(tail_x, low_dstate, 1, 1)
    d_c = dot(low_daff, low_b, 0, 0) + dot(fade_dy.astype(LOW), old_state.astype(LOW), 1, 1)
    skip_x = skip_ref[0:1, :] * inputs_x
    from_y = dy * (y_ref[...] - skip_x) - scaled_x * dx_wide
    dcum = dot(halves(from_y), gather)
    from_dt = dot(halves(inputs_x * dx_wide), gather)
    upper = jnp.where(causal, 1.0, 0.0).astype(F32)
    da = dot(upper, dcum, precision=PRECISE) + state_dot
    ddt = from_dt + head_ref[2:3, :] * da
    dpre_dt = ddt * jax.nn.sigmoid(pre_dt)
    skip_grad_ref[0:1, :] += jnp.sum(dy * inputs_x, axis=0, keepdims=True)
    head_grad_ref[0:1, :] += jnp.sum(dpre_dt, axis=0, keepdims=True)
    head_grad_ref[1:2, :] += head_ref[2:3, :] * jnp.sum(step_dt * da, axis=0, keepdims=True)
    dinputs = dt_wide * dx_wide + skip_ref[0:1, :] * dy
    dconv = jnp.concatenate([dinputs, d_b, d_c], axis=1) * slope
    dext[0:size, :] = dconv
    inner = ext[8 : 8 + size, :]
    du = conv_ref[3:4, :] * dconv
    conv_grad_ref[4:5, :] += jnp.sum(dconv, axis=0, keepdims=True)
    conv_grad_ref[3:4, :] += jnp.sum(inner * dconv, axis=0, keepdims=True)
    for tap in range(3):
        moved = dext[3 - tap : 3 - tap + size, :]
        du = du + conv_ref[tap : tap + 1, :] * moved
        conv_grad_ref[tap : tap + 1, :] += jnp.sum(inner * moved, axis=0, keepdims=True)
    dext[size : size + 8, :] = dconv[0:8, :]
    low_grad = jnp.concatenate([du.astype(LOW), dpre_dt.astype(LOW)], axis=1)
    low_dz = dz_ref[...]
    grad_ref[:, :width] = low_dz
    grad_ref[:, width:] = low_grad
    dnormed = dot(low_dz, z_weight_ref[...], 1, 1) + dot(low_grad, weight_ref[...], 1, 1)
    dnormed_ref[...] = dnormed.astype(LOW)


def whole(shape):
    return pl.BlockSpec(shape, lambda *_: (0,) * len(shape))


def params():
    return pltpu.CompilerParams(
        vmem_limit_bytes=VMEM_BYTES, dimension_semantics=("arbitrary",)
    )


def spread_matrix(head_count, width):
    lanes = jnp.arange(LANES)[:, None]
    heads = (jnp.arange(width) // HEAD_WIDTH)[None, :]
    once = (lanes == heads).astype(LOW)
    return jnp.concatenate([once, once], axis=0)


def position(block, me, count, blocks_per_piece):
    slot = (block // blocks_per_piece) ^ me
    half = count // blocks_per_piece // 2
    return ((slot % 2) * half + slot // 2) * blocks_per_piece + block % blocks_per_piece


def scan_forward(me, rows, weight, conv_par, head_vals, skip, spread, blocks_per_piece, cover):
    total, depth = rows.shape
    width = skip.shape[1]
    conv_width = conv_par.shape[1]
    count = total // BLOCK
    pre_width = weight.shape[1]
    state_size = (conv_width - width) // 2

    def place(step, me_ref):
        return position(step, me_ref[0], count, blocks_per_piece)

    def at(step, me_ref):
        return (place(step, me_ref), 0)

    return pl.pallas_call(
        scan_kernel,
        out_shape=(
            jax.ShapeDtypeStruct((total, pre_width), F32),
            jax.ShapeDtypeStruct((total, width), F32),
            jax.ShapeDtypeStruct((count, state_size, width), F32),
        ),
        grid_spec=pltpu.PrefetchScalarGridSpec(
            num_scalar_prefetch=1,
            grid=(count,),
            in_specs=[
                pl.BlockSpec((BLOCK, depth), at),
                whole(weight.shape),
                whole(conv_par.shape),
                whole(head_vals.shape),
                whole(skip.shape),
                whole(spread.shape),
            ],
            out_specs=[
                pl.BlockSpec((BLOCK, pre_width), at),
                pl.BlockSpec((BLOCK, width), at),
                pl.BlockSpec((1, state_size, width), lambda step, me_ref: (step, 0, 0)),
            ],
            scratch_shapes=[
                pltpu.VMEM((state_size, width), F32),
                pltpu.VMEM((BLOCK + 8, conv_width), F32),
            ],
        ),
        compiler_params=params(),
        cost_estimate=pl.CostEstimate(
            flops=int(cover * total * depth * pre_width),
            bytes_accessed=total * width,
            transcendentals=0,
        ),
        name="scan_forward",
    )(me, rows, weight, conv_par, head_vals, skip, spread)


def gate_forward(rows, y, gate_weight, gain, z_all, part, blocks_per_piece):
    total, depth = rows.shape
    width = y.shape[1]
    count = total // BLOCK // blocks_per_piece
    middle = count // 2
    earlier = () if z_all is None else (z_all,)

    def spot(step):
        return (step + middle) % count

    def at(step):
        return (spot(step) * blocks_per_piece + part, 0)

    return pl.pallas_call(
        gate_kernel,
        out_shape=(
            jax.ShapeDtypeStruct((total, width), F32),
            jax.ShapeDtypeStruct((middle * BLOCK, depth), LOW),
            jax.ShapeDtypeStruct((middle * BLOCK, depth), LOW),
            jax.ShapeDtypeStruct((count * BLOCK, 1), F32),
        ),
        grid=(count,),
        in_specs=[
            pl.BlockSpec((BLOCK, depth), at),
            pl.BlockSpec((BLOCK, width), at),
            pl.BlockSpec((depth, width), lambda step: (0, 0)),
            pl.BlockSpec((depth, width), lambda step: (0, 1)),
            whole(gain.shape),
            *[pl.BlockSpec(memory_space=pl.ANY) for _ in earlier],
        ],
        out_specs=[
            pl.BlockSpec((BLOCK, width), at),
            pl.BlockSpec((BLOCK, depth), lambda step: (jnp.minimum(step, middle - 1), 0)),
            pl.BlockSpec((BLOCK, depth), lambda step: (jnp.maximum(step - middle, 0), 0)),
            pl.BlockSpec((BLOCK, 1), lambda step: (spot(step), 0)),
        ],
        input_output_aliases={5: 0} if earlier else {},
        compiler_params=params(),
        cost_estimate=pl.CostEstimate(
            flops=16 * count * BLOCK * depth * width,
            bytes_accessed=count * BLOCK * (4 * depth + 8 * width),
            transcendentals=count * BLOCK * width,
        ),
        name="gate_forward",
    )(rows, y, gate_weight, gate_weight, gain, *earlier)


def gate_backward(grad_rows, y, gate_z, stats, gate_weight, gain):
    total, depth = grad_rows.shape
    width = y.shape[1]

    def at(step):
        return (step, 0)

    return pl.pallas_call(
        gate_back_kernel,
        out_shape=(
            jax.ShapeDtypeStruct((total, width), LOW),
            jax.ShapeDtypeStruct((total, width), F32),
            jax.ShapeDtypeStruct((total, width), LOW),
            jax.ShapeDtypeStruct((1, width), F32),
        ),
        grid=(total // BLOCK,),
        in_specs=[
            pl.BlockSpec((BLOCK, depth), at),
            pl.BlockSpec((BLOCK, width), at),
            pl.BlockSpec((BLOCK, width), at),
            pl.BlockSpec((BLOCK, 2), at),
            pl.BlockSpec((depth, width), lambda step: (0, 1)),
            whole(gain.shape),
        ],
        out_specs=[
            pl.BlockSpec((BLOCK, width), at),
            pl.BlockSpec((BLOCK, width), at),
            pl.BlockSpec((BLOCK, width), at),
            whole(gain.shape),
        ],
        compiler_params=params(),
        cost_estimate=pl.CostEstimate(
            flops=total * width, bytes_accessed=total * width, transcendentals=0,
        ),
        name="gate_backward",
    )(grad_rows, y, gate_z, stats, gate_weight, gain)


def scan_backward(
    me, dy, y, pre, kept, conv_par, head_vals, skip, spread, dz, gate_weight, weight, blocks_per_piece
):
    total, width = dy.shape
    pre_width = pre.shape[1]
    conv_width = conv_par.shape[1]
    state_size = kept.shape[1]
    count = total // BLOCK
    halo_blocks = BLOCK // 8
    gather = spread.T
    gather = jnp.concatenate([gather[:, :LANES]] * 2, axis=0)

    def place(block, me_ref):
        return position(block, me_ref[0], count, blocks_per_piece)

    def at(step, me_ref):
        return (place(count - 1 - step, me_ref), 0)

    def parted(step, me_ref):
        spot = place(count - 1 - step, me_ref)
        return ((spot % blocks_per_piece) * (count // blocks_per_piece) + spot // blocks_per_piece, 0)

    def before(step, me_ref):
        return (place(jnp.maximum(count - 2 - step, 0), me_ref) * halo_blocks + halo_blocks - 1, 0)

    return pl.pallas_call(
        scan_back_kernel,
        out_shape=(
            jax.ShapeDtypeStruct((total, width + pre_width), LOW),
            jax.ShapeDtypeStruct((total, weight.shape[0]), LOW),
            jax.ShapeDtypeStruct((8, conv_width), F32),
            jax.ShapeDtypeStruct((8, LANES), F32),
            jax.ShapeDtypeStruct((8, width), F32),
        ),
        grid_spec=pltpu.PrefetchScalarGridSpec(
            num_scalar_prefetch=1,
            grid=(count,),
            in_specs=[
                pl.BlockSpec((BLOCK, width), at),
                pl.BlockSpec((BLOCK, width), at),
                pl.BlockSpec((BLOCK, pre_width), at),
                pl.BlockSpec((8, pre_width), before),
                pl.BlockSpec((1, state_size, width), lambda step, me_ref: (count - 1 - step, 0, 0)),
                whole(conv_par.shape),
                whole(head_vals.shape),
                whole(skip.shape),
                whole(spread.shape),
                whole(gather.shape),
                pl.BlockSpec((BLOCK, width), at),
                pl.BlockSpec((weight.shape[0], width), lambda step, me_ref: (0, 0)),
                whole(weight.shape),
            ],
            out_specs=[
                pl.BlockSpec((BLOCK, width + pre_width), at),
                pl.BlockSpec((BLOCK, weight.shape[0]), parted),
                whole((8, conv_width)),
                whole((8, LANES)),
                whole((8, width)),
            ],
            scratch_shapes=[
                pltpu.VMEM((state_size, width), F32),
                pltpu.VMEM((BLOCK + 8, conv_width), F32),
                pltpu.VMEM((BLOCK + 8, conv_width), F32),
            ],
        ),
        compiler_params=params(),
        cost_estimate=pl.CostEstimate(
            flops=total * width, bytes_accessed=total * width, transcendentals=0,
        ),
        name="scan_backward",
    )(me, dy, y, pre, pre, kept, conv_par, head_vals, skip, spread, gather, dz, gate_weight, weight)


def root_kernel(rows_ref, root_ref):
    vals = rows_ref[...]
    root_ref[...] = lax.rsqrt(jnp.mean(vals * vals, axis=1, keepdims=True) + NORM_EPS)


def first_root(rows):
    return pl.pallas_call(
        root_kernel,
        out_shape=jax.ShapeDtypeStruct((rows.shape[0], 1), F32),
        compiler_params=pltpu.CompilerParams(vmem_limit_bytes=VMEM_BYTES),
        cost_estimate=pl.CostEstimate(flops=10**11, bytes_accessed=rows.size * 4, transcendentals=0),
        name="first_root",
    )(rows)


def swap(vals, distance, count):
    return lax.ppermute(vals, "tensor", [(src, src ^ distance) for src in range(count)])


def gather_pieces(own, count):
    far = swap(own, 2, count)
    return [own, far, swap(own, 1, count), swap(far, 1, count)]


def gather_slots(own, count, beside=None):
    far = swap(own, 2, count)
    if beside is not None:
        far, beside = lax.optimization_barrier((far, beside))
    full = jnp.concatenate([own, far, swap(own, 1, count), swap(far, 1, count)], axis=0)
    return full if beside is None else (full, beside)


def gather_parts(parts, kept, count):
    parts = list(parts)
    gathered = []
    for spot, part in enumerate(parts):
        far = swap(part, 2, count)
        if spot + 1 < len(parts):
            far, parts[spot + 1] = lax.optimization_barrier((far, parts[spot + 1]))
        gathered.append([kept[spot], far, swap(part, 1, count), swap(far, 1, count)])
    return jnp.concatenate([part[spot] for spot in range(count) for part in gathered], axis=0)


def reduce_slots(sent, held, count, wire):
    return reduce_far(reduce_near(sent, held, count, wire), count, wire)


def reduce_near(sent, held, count, wire):
    return held.astype(F32) + swap(sent.astype(wire), 1, count).astype(F32)


def reduce_far(near, count, wire):
    return add_far(near, swap_far(near, count, wire))


def swap_far(near, count, wire):
    return swap(near[near.shape[0] // 2 :].astype(wire), 2, count)


def add_far(near, far):
    return near[: far.shape[0]] + far.astype(F32)


def ring_index(place, count):
    return jnp.where(place < count // 2, 2 * place, 2 * (count - place) - 1)


def ring_place(index, count):
    return jnp.where(index % 2 == 0, index // 2, count - (index + 1) // 2)


def ring_step(vals, way, count):
    order = list(range(0, count, 2)) + list(range(count - 1, 0, -2))
    pairs = [(order[spot], order[(spot + way) % count]) for spot in range(count)]
    return lax.ppermute(vals, "dp", pairs)


class RingReduce:
    def __init__(self, vals, count):
        self.vals, self.count = vals, count
        self.share = vals.shape[0] // count
        self.place = ring_place(lax.axis_index("dp"), count)
        self.total_hops = count // 2
        self.hops = {1: count // 2, -1: count - 1 - count // 2}
        self.moving = {way: self.chunk(way * hops).astype(LOW) for way, hops in self.hops.items()}
        self.done = 0

    def chunk(self, offset):
        index = ring_index((self.place + offset) % self.count, self.count)
        return lax.dynamic_slice_in_dim(self.vals, index * self.share, self.share, 0).astype(F32)

    def hop(self):
        self.done += 1
        for way, hops in self.hops.items():
            if self.done > hops:
                continue
            moved = ring_step(self.moving[way], way, self.count)
            if self.done < hops:
                moved = (moved.astype(F32) + self.chunk(way * (hops - self.done))).astype(LOW)
            self.moving[way] = moved

    def finish(self):
        while self.done < self.total_hops:
            self.hop()
        return self.chunk(0) + self.moving[1].astype(F32) + self.moving[-1].astype(F32)


def xor_step(vals, axis, distance, count):
    return lax.ppermute(vals, axis, [(src, src ^ distance) for src in range(count)])


def xor_sum(vals, axis, count):
    distance = 1
    while distance < count:
        vals = vals + xor_step(vals, axis, distance, count)
        distance *= 2
    return vals


def xor_gather(own, dp_count, tensor_count):
    stack = own
    for axis, count in (("dp", dp_count), ("tensor", tensor_count)):
        distance = 1
        while distance < count:
            stack = jnp.concatenate([stack, xor_step(stack, axis, distance, count)], axis=0)
            distance *= 2
    total = dp_count * tensor_count
    spots = jnp.arange(total)
    owner = (lax.axis_index("dp") ^ (spots % dp_count)) * tensor_count + (
        lax.axis_index("tensor") ^ (spots // dp_count)
    )
    chosen = owner[None, :] == spots[:, None]
    return jnp.sum(jnp.where(chosen[:, :, None], stack[None], 0.0), axis=1)


def adam_update(current, gradient, moment_old, square_old, step_rate, decay_coef):
    moment_new = BETA_ONE * moment_old + (1.0 - BETA_ONE) * gradient
    square_new = BETA_TWO * square_old + (1.0 - BETA_TWO) * gradient * gradient
    moment_hat = moment_new / (1.0 - BETA_ONE**STEP)
    square_hat = square_new / (1.0 - BETA_TWO**STEP)
    updated = current - step_rate * (
        moment_hat / (jnp.sqrt(square_hat) + ADAM_EPS) + decay_coef * current
    )
    return (updated, moment_new, square_new)


def inv_rms(vals):
    return lax.rsqrt(jnp.mean(vals * vals, axis=1, keepdims=True) + NORM_EPS)


def pad_rows(vals, rows):
    return jnp.pad(vals, ((0, rows - vals.shape[0]), (0, 0)))


def pad_lanes(vals, lanes):
    return jnp.pad(vals, ((0, 0), (0, lanes - vals.shape[1])))


def local(
    dp_count,
    tensor_count,
    resid_in,
    cotangent,
    w_zx,
    w_bc,
    w_dt,
    w_out,
    chan_par,
    head_par,
    bc_par,
    norm_gain,
    zx_first,
    zx_second,
    bc_first,
    bc_second,
    dt_first,
    dt_second,
    out_first,
    out_second,
    chan_first,
    chan_second,
    head_first,
    head_second,
    bcpar_first,
    bcpar_second,
    gain_first,
    gain_second,
):
    layer_total, depth_share, _, width = w_zx.shape
    rows_own, depth = resid_in.shape
    head_count = w_dt.shape[2]
    state_two = w_bc.shape[2]
    conv_width = width + state_two
    tap_total = bc_par.shape[1]
    pieces = rows_own // BLOCK
    me_dp = lax.axis_index("dp")
    me_tensor = lax.axis_index("tensor")
    me = me_tensor.astype(jnp.int32).reshape((1,))
    place = me_dp * tensor_count + me_tensor

    gain_share, bcpar_share = norm_gain.shape[1], bc_par.shape[2]
    flat = jnp.concatenate([norm_gain.reshape(-1), bc_par.reshape(-1)])[None, :]
    bc_weights = lax.all_gather(w_bc.astype(LOW), "tensor", axis=1, tiled=True)
    bc_weights, opening = lax.optimization_barrier((bc_weights, resid_in))
    flat, opening = lax.optimization_barrier((flat, first_root(opening)))
    weights = []
    for layer in range(layer_total):
        scan_share = jnp.concatenate(
            [
                w_zx[layer, :, 1, :].astype(LOW),
                bc_weights[layer],
                pad_lanes(w_dt[layer].astype(LOW), LANES),
            ],
            axis=1,
        )
        gate_share = jnp.concatenate(
            [w_zx[layer, :, 0, :].astype(LOW), w_out[layer].T.astype(LOW)], axis=1
        )
        if layer == 0:
            small = xor_gather(flat, dp_count, tensor_count)
        scan_weight = lax.all_gather(scan_share, "dp", axis=0, tiled=True)
        gate_weight = lax.all_gather(gate_share, "dp", axis=0, tiled=True)
        weights.append((scan_weight, gate_weight))
    gain_len = layer_total * gain_share
    gain_all = small[:, :gain_len].reshape(-1, layer_total, gain_share)
    gain_all = gain_all.transpose(1, 0, 2).reshape(layer_total, depth)
    bcpar_all = small[:, gain_len:].reshape(-1, layer_total, tap_total, bcpar_share)
    bcpar_all = bcpar_all.transpose(1, 2, 0, 3).reshape(layer_total, tap_total, state_two)

    spread = spread_matrix(head_count, width)
    def in_parts(vals):
        return [vals[part * BLOCK : (part + 1) * BLOCK] for part in range(pieces)]

    def in_turn(far_list, make):
        made, ready = [], []
        for spot, far in enumerate(far_list):
            if spot:
                far, held = lax.optimization_barrier((far, made[-1][0]))
                ready.append(held)
            made.append(make(spot, far))
        ready.append(made[-1][0])
        return made, ready

    hidden = in_parts(resid_in)
    roots = in_parts(opening)
    low_rows = ready_rows = None
    kept = []
    for layer in range(layer_total):
        scan_weight, gate_weight = weights[layer]
        conv_par = pad_rows(jnp.concatenate([chan_par[layer, :-1], bcpar_all[layer]], axis=1), 8)
        decay = -jnp.exp(head_par[layer, 1])
        head_vals = pad_rows(
            pad_lanes(jnp.stack([head_par[layer, 0], decay * LOG2E, decay], 0), LANES), 8
        )
        skip = pad_rows(jnp.repeat(head_par[layer, 2], HEAD_WIDTH)[None, :], 8)
        gain_q = chan_par[layer, -1:]
        if layer == 0:
            normed = (resid_in * opening * gain_all[layer][None, :]).astype(LOW)
            rows, scan_weight = gather_slots(normed, tensor_count, scan_weight)
            weights[0] = (scan_weight, gate_weight)
            rows, first_grad = lax.optimization_barrier((rows, cotangent.astype(LOW)))
            first_far = swap(first_grad, 2, tensor_count)
        else:
            rows = gather_parts(low_rows, ready_rows, tensor_count)
        pre, y, states = scan_forward(
            me, rows, scan_weight, conv_par, head_vals, skip, spread, pieces, 0.1 if layer else 8.0
        )
        if layer == 0:
            y, first_far = lax.optimization_barrier((y, first_far))
            first_full = jnp.concatenate(
                [first_grad, first_far, swap(first_grad, 1, tensor_count), swap(first_far, 1, tensor_count)], axis=0
            )
            y, first_full = lax.optimization_barrier((y, first_full))
        gate_z = None
        near_list, square_list = [], []
        for part in range(pieces):
            gate_z, sent, held, squares = gate_forward(rows, y, gate_weight, gain_q, gate_z, part, pieces)
            near_list.append(reduce_near(sent, held, tensor_count, LOW))
            square_list.append(squares)
        middle = square_list[0].shape[0] // 2
        square_sent = jnp.concatenate(
            [vals[middle + spot : middle + spot + BLOCK] for spot in range(0, middle, BLOCK) for vals in square_list]
        )
        square_held = jnp.concatenate(
            [vals[spot : spot + BLOCK] for spot in range(0, middle, BLOCK) for vals in square_list]
        )
        square_own = reduce_slots(square_sent, square_held, tensor_count, F32)
        near_list, square_own = lax.optimization_barrier((near_list, square_own))
        inv_list = in_parts(lax.rsqrt(square_own / INNER + NORM_EPS))
        far_list = [swap_far(near, tensor_count, LOW) for near in near_list]
        next_gain = gain_all[min(layer + 1, layer_total - 1)][None, :]

        def next_rows(spot, far, near_list=near_list, inv_list=inv_list, hidden=hidden, next_gain=next_gain):
            branch = add_far(near_list[spot], far)
            out = hidden[spot] + inv_list[spot] * branch
            root = inv_rms(out)
            return (out * root * next_gain).astype(LOW), out, root, branch

        made, ready_rows = in_turn(far_list, next_rows)
        kept.append(
            (
                hidden, roots, rows, pre, y, states, gate_z, inv_list, [entry[3] for entry in made],
                conv_par, head_vals, skip, gain_q,
            )
        )
        low_rows = [entry[0] for entry in made]
        hidden = [entry[1] for entry in made]
        roots = [entry[2] for entry in made]

    grad_hidden = in_parts(cotangent)
    zx_list = [None] * layer_total
    dt_list = [None] * layer_total
    out_list = [None] * layer_total
    bc_list = [None] * layer_total
    small_list = [None] * layer_total
    shared_list = [None] * layer_total
    gain_list = [None] * layer_total
    def place_scan(layer, total):
        z_sum, scan_sum = total[:, :width], total[:, width:]
        zx_list[layer] = jnp.stack([z_sum, scan_sum[:, :width]], axis=1)
        share = depth_share // tensor_count
        parts = [
            lax.dynamic_slice_in_dim(scan_sum[:, width:conv_width], (me_tensor ^ slot) * share, share, 0)
            for slot in [*range(0, tensor_count, 2), *range(1, tensor_count, 2)]
        ]
        middle = tensor_count // 2
        bc_list[layer] = reduce_slots(
            jnp.concatenate(parts[middle:], axis=0), jnp.concatenate(parts[:middle], axis=0), tensor_count, F32
        )
        dt_list[layer] = scan_sum[:, conv_width : conv_width + head_count]

    late = ()

    def owned(grad):
        return lax.psum_scatter(grad, "dp", scatter_dimension=0, tiled=True)

    for layer in reversed(range(layer_total)):
        scan_weight, gate_weight = weights[layer]
        (
            entering, roots, rows, pre, y, states, gate_z, inv_list, projected, conv_par, head_vals, skip, gain_q,
        ) = kept[layer]
        if layer == layer_total - 1:
            branch_low = [part.astype(LOW) for part in grad_hidden]
        stats = [
            jnp.concatenate([inv, jnp.sum(low.astype(F32) * branch, axis=1, keepdims=True)], axis=1)
            for inv, low, branch in zip(inv_list, branch_low, projected)
        ]
        stats = gather_slots(jnp.concatenate(stats, axis=0), tensor_count)
        full_grad = first_full if layer == layer_total - 1 else gather_parts(branch_low, ready_low, tensor_count)
        dz, dy, scaled, gain_five = gate_backward(full_grad, y, gate_z, stats, gate_weight, gain_q)
        out_grad = dot(full_grad, scaled, 0, 0).astype(LOW)
        dy, out_grad = lax.optimization_barrier((dy, out_grad))
        if layer + 1 < layer_total:
            late, out_grad = lax.optimization_barrier((late, out_grad))
        out_sum = owned(out_grad)
        dmerged, dnormed, conv_grad, head_grad, skip_grad = scan_backward(
            me, dy, y, pre, states, conv_par, head_vals, skip, spread, dz, gate_weight, scan_weight, pieces
        )
        out_sum, dnormed, dmerged = lax.optimization_barrier((out_sum, dnormed, dmerged))
        part_rows = dnormed.shape[0] // pieces
        near_list = []
        for part in range(pieces):
            vals = dnormed[part * part_rows : (part + 1) * part_rows]
            near_list.append(
                reduce_near(vals[part_rows // 2 :], vals[: part_rows // 2], tensor_count, LOW)
            )
        merged_grad = dot(rows, dmerged, 0, 0)
        if layer == 0:
            near_list, merged_grad = lax.optimization_barrier((near_list, merged_grad))
        far_list = [swap_far(near, tensor_count, LOW) for near in near_list]
        if layer == 0:
            ring = RingReduce(merged_grad, dp_count)
            ring.hop()
            rest = (conv_grad, head_grad, skip_grad, gain_five, out_sum, late)
            ring.moving, rest = lax.optimization_barrier((ring.moving, rest))
            conv_grad, head_grad, skip_grad, gain_five, out_sum, late = rest
            if layer + 1 < layer_total:
                place_scan(layer + 1, late.astype(F32))
            place_scan(layer, ring.finish())
        else:
            far_list[-1], merged_grad = lax.optimization_barrier((far_list[-1], merged_grad.astype(LOW)))
            late = owned(merged_grad)
        out_list[layer] = out_sum.astype(F32).T
        gain = gain_all[layer][None, :]

        def next_grad(
            spot, far, near_list=near_list, entering=entering, roots=roots, grad_hidden=grad_hidden, gain=gain
        ):
            part_grad = add_far(near_list[spot], far)
            part_in, root = entering[spot], roots[spot]
            gained = part_grad * gain
            shift = jnp.mean(gained * part_in, axis=1, keepdims=True) * root * root * root
            out = grad_hidden[spot] + root * gained - part_in * shift
            return out.astype(LOW), out, jnp.sum(part_grad * part_in * root, axis=0)

        made, ready_low = in_turn(far_list, next_grad)
        branch_low = [entry[0] for entry in made]
        grad_hidden = [entry[1] for entry in made]
        gain_grad = sum(entry[2] for entry in made)

        chan_grad = jnp.concatenate([conv_grad[:5, :width], gain_five], axis=0)
        skip_sum = skip_grad[0].reshape(head_count, HEAD_WIDTH).sum(axis=1)
        head_all = jnp.concatenate(
            [head_grad[0, :head_count], head_grad[1, :head_count], skip_sum]
        )
        small_list[layer] = jnp.concatenate([chan_grad.reshape(-1), head_all])
        gain_list[layer] = gain_grad
        shared_list[layer] = conv_grad[:5, width:].reshape(-1)

    shared = xor_sum(jnp.stack(shared_list, 0), "tensor", tensor_count)
    both = xor_sum(jnp.concatenate([jnp.stack(small_list, 0), shared], axis=1), "dp", dp_count)
    chan_len = chan_par.shape[1] * width
    head_len = head_par.shape[1] * head_count
    chan_stack = both[:, :chan_len].reshape(chan_par.shape)
    head_stack = both[:, chan_len : chan_len + head_len].reshape(head_par.shape)
    shared = both[:, chan_len + head_len :]
    gains = xor_sum(xor_sum(jnp.stack(gain_list, 0), "tensor", tensor_count), "dp", dp_count)
    gain_stack = lax.dynamic_slice_in_dim(gains, place * gain_share, gain_share, axis=1)
    bcpar_stack = lax.dynamic_slice_in_dim(
        shared.reshape(layer_total, tap_total, state_two), place * bcpar_share, bcpar_share, axis=2
    )

    zx_stack = with_layout_constraint(jnp.stack(zx_list, 0), Layout((0, 1, 2, 3)))
    zx_new = adam_update(w_zx, zx_stack, zx_first, zx_second, MATRIX_RATE, MATRIX_DECAY)
    bc_new = adam_update(w_bc, jnp.stack(bc_list, 0), bc_first, bc_second, MATRIX_RATE, MATRIX_DECAY)
    dt_new = adam_update(w_dt, jnp.stack(dt_list, 0), dt_first, dt_second, MATRIX_RATE, MATRIX_DECAY)
    out_new = adam_update(w_out, jnp.stack(out_list, 0), out_first, out_second, MATRIX_RATE, MATRIX_DECAY)
    chan_new = adam_update(chan_par, chan_stack, chan_first, chan_second, SMALL_RATE, 0.0)
    head_new = adam_update(head_par, head_stack, head_first, head_second, HEAD_RATE, 0.0)
    bcpar_new = adam_update(bc_par, bcpar_stack, bcpar_first, bcpar_second, SMALL_RATE, 0.0)
    gain_new = adam_update(norm_gain, gain_stack, gain_first, gain_second, SMALL_RATE, 0.0)
    return (
        jnp.concatenate(hidden, axis=0), jnp.concatenate(grad_hidden, axis=0), *zx_new, *bc_new, *dt_new, *out_new, *chan_new, *head_new, *bcpar_new, *gain_new,
    )


def solution(mesh):
    in_specs = (
        P(("dp", "tensor"), None),
        P(("dp", "tensor"), None),
        P(None, "dp", None, "tensor"),
        P(None, ("dp", "tensor"), None),
        P(None, "dp", "tensor"),
        P(None, "tensor", "dp"),
        P(None, None, "tensor"),
        P(None, None, "tensor"),
        P(None, None, ("dp", "tensor")),
        P(None, ("dp", "tensor")),
        P(None, "dp", None, "tensor"),
        P(None, "dp", None, "tensor"),
        P(None, ("dp", "tensor"), None),
        P(None, ("dp", "tensor"), None),
        P(None, "dp", "tensor"),
        P(None, "dp", "tensor"),
        P(None, "tensor", "dp"),
        P(None, "tensor", "dp"),
        P(None, None, "tensor"),
        P(None, None, "tensor"),
        P(None, None, "tensor"),
        P(None, None, "tensor"),
        P(None, None, ("dp", "tensor")),
        P(None, None, ("dp", "tensor")),
        P(None, ("dp", "tensor")),
        P(None, ("dp", "tensor")),
    )
    out_specs = (
        P(("dp", "tensor"), None),
        P(("dp", "tensor"), None),
        P(None, "dp", None, "tensor"),
        P(None, "dp", None, "tensor"),
        P(None, "dp", None, "tensor"),
        P(None, ("dp", "tensor"), None),
        P(None, ("dp", "tensor"), None),
        P(None, ("dp", "tensor"), None),
        P(None, "dp", "tensor"),
        P(None, "dp", "tensor"),
        P(None, "dp", "tensor"),
        P(None, "tensor", "dp"),
        P(None, "tensor", "dp"),
        P(None, "tensor", "dp"),
        P(None, None, "tensor"),
        P(None, None, "tensor"),
        P(None, None, "tensor"),
        P(None, None, "tensor"),
        P(None, None, "tensor"),
        P(None, None, "tensor"),
        P(None, None, ("dp", "tensor")),
        P(None, None, ("dp", "tensor")),
        P(None, None, ("dp", "tensor")),
        P(None, ("dp", "tensor")),
        P(None, ("dp", "tensor")),
        P(None, ("dp", "tensor")),
    )
    return jax.shard_map(
        functools.partial(local, mesh.shape["dp"], mesh.shape["tensor"]), mesh=mesh, in_specs=in_specs, out_specs=out_specs, check_vma=False)
```

```python
import functools
import math

import jax
import jax.numpy as jnp
from jax import lax
from jax.experimental import pallas as pl
from jax.experimental.layout import Layout, with_layout_constraint
from jax.experimental.pallas import tpu as pltpu
from jax.sharding import PartitionSpec as P

BLOCK = 256
STEP = 10
INNER = 3072
LANES = 128
HEAD_WIDTH = 64

NORM_EPS = 1e-05
BETA_ONE = 0.9
BETA_TWO = 0.95
ADAM_EPS = 1e-08
MATRIX_RATE = 0.02
MATRIX_DECAY = 0.1
SMALL_RATE = 0.3
HEAD_RATE = 2.0
PRECISE = lax.Precision.HIGHEST
LOG2E = math.log2(math.e)
LOW = jnp.bfloat16
F32 = jnp.float32
VMEM_BYTES = 56 * 1024 * 1024


def dot(left, right, left_dim=1, right_dim=0, precision=None):
    return lax.dot_general(
        left,
        right,
        (((left_dim,), (right_dim,)), ((), ())),
        preferred_element_type=F32,
        precision=precision,
    )


def split(vals):
    high = vals.astype(LOW)
    return high, (vals - high.astype(F32)).astype(LOW)


def halves(vals):
    return jnp.concatenate(split(vals), axis=1)


def left_parts(vals, axis):
    high, low = split(vals)
    return jnp.concatenate([high, low, high], axis=axis)


def right_parts(vals, axis):
    high, low = split(vals)
    return jnp.concatenate([high, high, low], axis=axis)


def mix_pair(mixing, pair):
    out = dot(jnp.concatenate(split(mixing), axis=1), jnp.concatenate([pair, pair], axis=0))
    return out[:, :LANES] + out[:, LANES:]


def softplus(vals):
    return jnp.maximum(vals, 0.0) + jnp.log1p(jnp.exp(-jnp.abs(vals)))


def conv_block(ext, conv_ref):
    rows = ext.shape[0] - 8
    total = conv_ref[4:5, :] + conv_ref[3:4, :] * ext[8 : 8 + rows, :]
    for tap in range(3):
        total = total + conv_ref[tap : tap + 1, :] * ext[5 + tap : 5 + tap + rows, :]
    return total


def decay_sums(step_dt, head_ref):
    size = step_dt.shape[0]
    row = lax.broadcasted_iota(jnp.int32, (size, size), 0)
    col = lax.broadcasted_iota(jnp.int32, (size, size), 1)
    lower = jnp.where(row >= col, 1.0, 0.0).astype(F32)
    return dot(lower, step_dt * head_ref[1:2, :], precision=PRECISE)


def scan_kernel(
    me_ref, rows_ref, weight_ref, conv_ref, head_ref, skip_ref, spread_ref,
    pre_ref, y_ref, kept_ref, state, ext,
):
    width = y_ref.shape[1]
    conv_width = ext.shape[1]
    half = (conv_width - width) // 2
    size = rows_ref.shape[0]

    @pl.when(pl.program_id(0) == 0)
    def _():
        state[...] = jnp.zeros_like(state)
        ext[0:8, :] = jnp.zeros((8, conv_width), F32)

    @pl.when(pl.program_id(0) > 0)
    def _():
        ext[0:8, :] = ext[size : size + 8, :]

    pre = dot(rows_ref[...], weight_ref[...])
    pre_ref[...] = pre
    ext[8 : 8 + size, :] = pre[:, :conv_width]
    conv = conv_block(ext, conv_ref)
    act = conv * jax.nn.sigmoid(conv)
    inputs_x = act[:, :width]
    left_c = left_parts(act[:, width + half :], 1)
    step_dt = softplus(pre[:, conv_width:] + head_ref[0:1, :])
    cum = decay_sums(step_dt, head_ref)
    cum_t = cum.T
    last = cum[size - 1 : size, :]
    spread = spread_ref[...]
    dt_wide = dot(halves(step_dt), spread)
    cum_wide = dot(halves(jnp.exp2(cum)), spread)
    tail_wide = dot(halves(jnp.exp2(last - cum)), spread)
    scaled_x = inputs_x * dt_wide
    high_x, low_x = split(scaled_x)
    row = lax.broadcasted_iota(jnp.int32, (size, size), 0)
    col = lax.broadcasted_iota(jnp.int32, (size, size), 1)
    affinity = jnp.where(row >= col, dot(left_c, right_parts(act[:, width : width + half], 1), 1, 1), 0.0)
    old_state = state[...]
    kept_ref[0] = old_state
    y_ref[...] = (
        cum_wide * dot(left_c, right_parts(old_state, 0)) + skip_ref[0:1, :] * inputs_x
    )
    state[...] = cum_wide[size - 1 : size, :] * old_state + dot(
        left_parts(act[:, width : width + half], 0), right_parts(scaled_x * tail_wide, 0), 0, 0
    )
    first_half = lax.broadcasted_iota(jnp.int32, (size, LANES), 1) < HEAD_WIDTH
    for pair in range(width // LANES):
        cols = slice(pair * LANES, (pair + 1) * LANES)
        pair_x = jnp.concatenate([high_x[:, cols], low_x[:, cols]], axis=1)
        parts = []
        for head in (2 * pair, 2 * pair + 1):
            gap = cum[:, head : head + 1] - cum_t[head : head + 1, :]
            parts.append(mix_pair(affinity * jnp.exp2(jnp.minimum(gap, 0.0)), pair_x))
        y_ref[:, cols] += jnp.where(first_half, parts[0], parts[1])


def gate_kernel(rows_ref, y_ref, z_weight_ref, out_weight_ref, gain_ref, *refs):
    z_ref, sent_ref, own_ref, sq_ref = refs[-4:]
    gate_z = dot(rows_ref[...], z_weight_ref[...])
    z_ref[...] = gate_z
    gated = y_ref[...] * (gate_z * jax.nn.sigmoid(gate_z))
    sq_ref[...] = jnp.sum(gated * gated, axis=1, keepdims=True)
    low_gated = (gated * gain_ref[...]).astype(LOW)
    partial = dot(low_gated, out_weight_ref[...], 1, 1).astype(LOW)
    sending = pl.program_id(0) < pl.num_programs(0) // 2

    @pl.when(sending)
    def _():
        sent_ref[...] = partial

    @pl.when(jnp.logical_not(sending))
    def _():
        own_ref[...] = partial


def gate_back_kernel(
    grad_ref, y_ref, z_ref, stat_ref, out_weight_ref, gain_ref,
    dz_ref, dy_ref, scaled_ref, gain_grad_ref,
):
    @pl.when(pl.program_id(0) == 0)
    def _():
        gain_grad_ref[...] = jnp.zeros_like(gain_grad_ref)

    dscaled = dot(grad_ref[...], out_weight_ref[...])
    gate_z = z_ref[...]
    y = y_ref[...]
    gain = gain_ref[...]
    inv = stat_ref[:, 0:1]
    shift = stat_ref[:, 1:2] * inv * inv * inv * (1.0 / INNER)
    sig = jax.nn.sigmoid(gate_z)
    silu_z = gate_z * sig
    gated = y * silu_z
    normed = gated * inv
    scaled_ref[...] = (normed * gain).astype(LOW)
    gain_grad_ref[...] += jnp.sum(dscaled * normed, axis=0, keepdims=True)
    dgated = inv * gain * dscaled - gated * shift
    dz_ref[...] = (dgated * y * (sig + silu_z * (1.0 - sig))).astype(LOW)
    dy_ref[...] = dgated * silu_z


def scan_back_kernel(
    me_ref, dy_ref, y_ref, pre_ref, halo_ref, kept_ref, conv_ref, head_ref, skip_ref,
    spread_ref, gather_ref, dz_ref, z_weight_ref, weight_ref,
    grad_ref, dnormed_ref, conv_grad_ref, head_grad_ref, skip_grad_ref,
    dstate, ext, dext,
):
    size, width = dy_ref.shape
    conv_width = ext.shape[1]
    half = (conv_width - width) // 2
    step = pl.program_id(0)
    last_step = pl.num_programs(0) - 1

    @pl.when(step == 0)
    def _():
        dstate[...] = jnp.zeros_like(dstate)
        dext[size : size + 8, :] = jnp.zeros((8, conv_width), F32)
        conv_grad_ref[...] = jnp.zeros_like(conv_grad_ref)
        head_grad_ref[...] = jnp.zeros_like(head_grad_ref)
        skip_grad_ref[...] = jnp.zeros_like(skip_grad_ref)

    ext[0:8, :] = jnp.where(step == last_step, 0.0, halo_ref[:, :conv_width])
    ext[8 : 8 + size, :] = pre_ref[:, :conv_width]
    conv = conv_block(ext, conv_ref)
    sig = jax.nn.sigmoid(conv)
    act = conv * sig
    slope = sig + act * (1.0 - sig)
    inputs_x = act[:, :width]
    full_b = act[:, width : width + half]
    full_c = act[:, width + half :]
    low_b = full_b.astype(LOW)
    low_c = full_c.astype(LOW)
    left_b = left_parts(full_b, 1)
    pre_dt = pre_ref[:, conv_width:] + head_ref[0:1, :]
    step_dt = softplus(pre_dt)
    cum = decay_sums(step_dt, head_ref)
    cum_t = cum.T
    last = cum[size - 1 : size, :]
    spread = spread_ref[...]
    gather = gather_ref[...]
    dt_wide = dot(halves(step_dt), spread)
    cum_wide = dot(halves(jnp.exp2(cum)), spread)
    tail_wide = dot(halves(jnp.exp2(last - cum)), spread)
    scaled_x = inputs_x * dt_wide
    low_x = scaled_x.astype(LOW)
    tail_x = (scaled_x * tail_wide).astype(LOW)
    dy = dy_ref[...]
    high_dy, low_dy = split(dy)
    fade_dy = dy * cum_wide
    old_state = kept_ref[0]
    out_dstate = dstate[...]
    low_dstate = out_dstate.astype(LOW)
    tail_dx = tail_wide * dot(left_b, right_parts(out_dstate, 0))
    decay_all = cum_wide[size - 1 : size, :]
    state_sum = jnp.sum(old_state * out_dstate, axis=0, keepdims=True) * decay_all
    state_sum = state_sum + jnp.sum(scaled_x * tail_dx, axis=0, keepdims=True)
    state_dot = dot(halves(state_sum * jnp.ones((8, 1), F32)), gather)[0:1, :]
    dstate[...] = decay_all * out_dstate + dot(
        left_parts(full_c, 0), right_parts(fade_dy, 0), 0, 0
    )

    row = lax.broadcasted_iota(jnp.int32, (size, size), 0)
    col = lax.broadcasted_iota(jnp.int32, (size, size), 1)
    causal = col >= row
    affinity = jnp.where(causal, dot(left_b, right_parts(full_c, 1), 1, 1), 0.0)
    first_half = lax.broadcasted_iota(jnp.int32, (size, LANES), 1) < HEAD_WIDTH
    daffinity = jnp.zeros((size, size), F32)
    parts = []
    for pair in range(width // LANES):
        cols = slice(pair * LANES, (pair + 1) * LANES)
        pair_x = low_x[:, cols]
        pair_dy = high_dy[:, cols]
        both_dy = jnp.concatenate([pair_dy, low_dy[:, cols]], axis=1)
        zero = jnp.zeros_like(pair_x)
        here = []
        for which, head in enumerate((2 * pair, 2 * pair + 1)):
            gap = cum_t[head : head + 1, :] - cum[:, head : head + 1]
            fading = jnp.exp2(jnp.minimum(gap, 0.0))
            own_x = jnp.where(first_half, pair_x, zero) if which == 0 else jnp.where(first_half, zero, pair_x)
            daffinity = daffinity + fading * dot(own_x, pair_dy, 1, 1)
            here.append(mix_pair(affinity * fading, both_dy))
        parts.append(jnp.where(first_half, here[0], here[1]))
    low_daff = jnp.where(causal, daffinity, 0.0).astype(LOW)
    dx_wide = jnp.concatenate(parts, axis=1) + tail_dx
    d_b = dot(low_daff, low_c) + dot(tail_x, low_dstate, 1, 1)
    d_c = dot(low_daff, low_b, 0, 0) + dot(fade_dy.astype(LOW), old_state.astype(LOW), 1, 1)
    skip_x = skip_ref[0:1, :] * inputs_x
    from_y = dy * (y_ref[...] - skip_x) - scaled_x * dx_wide
    dcum = dot(halves(from_y), gather)
    from_dt = dot(halves(inputs_x * dx_wide), gather)
    upper = jnp.where(causal, 1.0, 0.0).astype(F32)
    da = dot(upper, dcum, precision=PRECISE) + state_dot
    ddt = from_dt + head_ref[2:3, :] * da
    dpre_dt = ddt * jax.nn.sigmoid(pre_dt)
    skip_grad_ref[0:1, :] += jnp.sum(dy * inputs_x, axis=0, keepdims=True)
    head_grad_ref[0:1, :] += jnp.sum(dpre_dt, axis=0, keepdims=True)
    head_grad_ref[1:2, :] += head_ref[2:3, :] * jnp.sum(step_dt * da, axis=0, keepdims=True)
    dinputs = dt_wide * dx_wide + skip_ref[0:1, :] * dy
    dconv = jnp.concatenate([dinputs, d_b, d_c], axis=1) * slope
    dext[0:size, :] = dconv
    inner = ext[8 : 8 + size, :]
    du = conv_ref[3:4, :] * dconv
    conv_grad_ref[4:5, :] += jnp.sum(dconv, axis=0, keepdims=True)
    conv_grad_ref[3:4, :] += jnp.sum(inner * dconv, axis=0, keepdims=True)
    for tap in range(3):
        moved = dext[3 - tap : 3 - tap + size, :]
        du = du + conv_ref[tap : tap + 1, :] * moved
        conv_grad_ref[tap : tap + 1, :] += jnp.sum(inner * moved, axis=0, keepdims=True)
    dext[size : size + 8, :] = dconv[0:8, :]
    low_grad = jnp.concatenate([du.astype(LOW), dpre_dt.astype(LOW)], axis=1)
    low_dz = dz_ref[...]
    grad_ref[:, :width] = low_dz
    grad_ref[:, width:] = low_grad
    dnormed = dot(low_dz, z_weight_ref[...], 1, 1) + dot(low_grad, weight_ref[...], 1, 1)
    dnormed_ref[...] = dnormed.astype(LOW)


def whole(shape):
    return pl.BlockSpec(shape, lambda *_: (0,) * len(shape))


def params():
    return pltpu.CompilerParams(
        vmem_limit_bytes=VMEM_BYTES, dimension_semantics=("arbitrary",)
    )


def spread_matrix(head_count, width):
    lanes = jnp.arange(LANES)[:, None]
    heads = (jnp.arange(width) // HEAD_WIDTH)[None, :]
    once = (lanes == heads).astype(LOW)
    return jnp.concatenate([once, once], axis=0)


def position(block, me, count, blocks_per_piece):
    slot = (block // blocks_per_piece) ^ me
    half = count // blocks_per_piece // 2
    return ((slot % 2) * half + slot // 2) * blocks_per_piece + block % blocks_per_piece


def scan_forward(me, rows, weight, conv_par, head_vals, skip, spread, blocks_per_piece, cover):
    total, depth = rows.shape
    width = skip.shape[1]
    conv_width = conv_par.shape[1]
    count = total // BLOCK
    pre_width = weight.shape[1]
    state_size = (conv_width - width) // 2

    def place(step, me_ref):
        return position(step, me_ref[0], count, blocks_per_piece)

    def at(step, me_ref):
        return (place(step, me_ref), 0)

    return pl.pallas_call(
        scan_kernel,
        out_shape=(
            jax.ShapeDtypeStruct((total, pre_width), F32),
            jax.ShapeDtypeStruct((total, width), F32),
            jax.ShapeDtypeStruct((count, state_size, width), F32),
        ),
        grid_spec=pltpu.PrefetchScalarGridSpec(
            num_scalar_prefetch=1,
            grid=(count,),
            in_specs=[
                pl.BlockSpec((BLOCK, depth), at),
                whole(weight.shape),
                whole(conv_par.shape),
                whole(head_vals.shape),
                whole(skip.shape),
                whole(spread.shape),
            ],
            out_specs=[
                pl.BlockSpec((BLOCK, pre_width), at),
                pl.BlockSpec((BLOCK, width), at),
                pl.BlockSpec((1, state_size, width), lambda step, me_ref: (step, 0, 0)),
            ],
            scratch_shapes=[
                pltpu.VMEM((state_size, width), F32),
                pltpu.VMEM((BLOCK + 8, conv_width), F32),
            ],
        ),
        compiler_params=params(),
        cost_estimate=pl.CostEstimate(
            flops=int(cover * total * depth * pre_width),
            bytes_accessed=total * width,
            transcendentals=0,
        ),
        name="scan_forward",
    )(me, rows, weight, conv_par, head_vals, skip, spread)


def gate_forward(rows, y, gate_weight, gain, z_all, part, blocks_per_piece):
    total, depth = rows.shape
    width = y.shape[1]
    count = total // BLOCK // blocks_per_piece
    middle = count // 2
    earlier = () if z_all is None else (z_all,)

    def spot(step):
        return (step + middle) % count

    def at(step):
        return (spot(step) * blocks_per_piece + part, 0)

    return pl.pallas_call(
        gate_kernel,
        out_shape=(
            jax.ShapeDtypeStruct((total, width), F32),
            jax.ShapeDtypeStruct((middle * BLOCK, depth), LOW),
            jax.ShapeDtypeStruct((middle * BLOCK, depth), LOW),
            jax.ShapeDtypeStruct((count * BLOCK, 1), F32),
        ),
        grid=(count,),
        in_specs=[
            pl.BlockSpec((BLOCK, depth), at),
            pl.BlockSpec((BLOCK, width), at),
            pl.BlockSpec((depth, width), lambda step: (0, 0)),
            pl.BlockSpec((depth, width), lambda step: (0, 1)),
            whole(gain.shape),
            *[pl.BlockSpec(memory_space=pl.ANY) for _ in earlier],
        ],
        out_specs=[
            pl.BlockSpec((BLOCK, width), at),
            pl.BlockSpec((BLOCK, depth), lambda step: (jnp.minimum(step, middle - 1), 0)),
            pl.BlockSpec((BLOCK, depth), lambda step: (jnp.maximum(step - middle, 0), 0)),
            pl.BlockSpec((BLOCK, 1), lambda step: (spot(step), 0)),
        ],
        input_output_aliases={5: 0} if earlier else {},
        compiler_params=params(),
        cost_estimate=pl.CostEstimate(
            flops=16 * count * BLOCK * depth * width,
            bytes_accessed=count * BLOCK * (4 * depth + 8 * width),
            transcendentals=count * BLOCK * width,
        ),
        name="gate_forward",
    )(rows, y, gate_weight, gate_weight, gain, *earlier)


def gate_backward(grad_rows, y, gate_z, stats, gate_weight, gain):
    total, depth = grad_rows.shape
    width = y.shape[1]

    def at(step):
        return (step, 0)

    return pl.pallas_call(
        gate_back_kernel,
        out_shape=(
            jax.ShapeDtypeStruct((total, width), LOW),
            jax.ShapeDtypeStruct((total, width), F32),
            jax.ShapeDtypeStruct((total, width), LOW),
            jax.ShapeDtypeStruct((1, width), F32),
        ),
        grid=(total // BLOCK,),
        in_specs=[
            pl.BlockSpec((BLOCK, depth), at),
            pl.BlockSpec((BLOCK, width), at),
            pl.BlockSpec((BLOCK, width), at),
            pl.BlockSpec((BLOCK, 2), at),
            pl.BlockSpec((depth, width), lambda step: (0, 1)),
            whole(gain.shape),
        ],
        out_specs=[
            pl.BlockSpec((BLOCK, width), at),
            pl.BlockSpec((BLOCK, width), at),
            pl.BlockSpec((BLOCK, width), at),
            whole(gain.shape),
        ],
        compiler_params=params(),
        cost_estimate=pl.CostEstimate(
            flops=total * width, bytes_accessed=total * width, transcendentals=0,
        ),
        name="gate_backward",
    )(grad_rows, y, gate_z, stats, gate_weight, gain)


def scan_backward(
    me, dy, y, pre, kept, conv_par, head_vals, skip, spread, dz, gate_weight, weight, blocks_per_piece
):
    total, width = dy.shape
    pre_width = pre.shape[1]
    conv_width = conv_par.shape[1]
    state_size = kept.shape[1]
    count = total // BLOCK
    halo_blocks = BLOCK // 8
    gather = spread.T
    gather = jnp.concatenate([gather[:, :LANES]] * 2, axis=0)

    def place(block, me_ref):
        return position(block, me_ref[0], count, blocks_per_piece)

    def at(step, me_ref):
        return (place(count - 1 - step, me_ref), 0)

    def parted(step, me_ref):
        spot = place(count - 1 - step, me_ref)
        return ((spot % blocks_per_piece) * (count // blocks_per_piece) + spot // blocks_per_piece, 0)

    def before(step, me_ref):
        return (place(jnp.maximum(count - 2 - step, 0), me_ref) * halo_blocks + halo_blocks - 1, 0)

    return pl.pallas_call(
        scan_back_kernel,
        out_shape=(
            jax.ShapeDtypeStruct((total, width + pre_width), LOW),
            jax.ShapeDtypeStruct((total, weight.shape[0]), LOW),
            jax.ShapeDtypeStruct((8, conv_width), F32),
            jax.ShapeDtypeStruct((8, LANES), F32),
            jax.ShapeDtypeStruct((8, width), F32),
        ),
        grid_spec=pltpu.PrefetchScalarGridSpec(
            num_scalar_prefetch=1,
            grid=(count,),
            in_specs=[
                pl.BlockSpec((BLOCK, width), at),
                pl.BlockSpec((BLOCK, width), at),
                pl.BlockSpec((BLOCK, pre_width), at),
                pl.BlockSpec((8, pre_width), before),
                pl.BlockSpec((1, state_size, width), lambda step, me_ref: (count - 1 - step, 0, 0)),
                whole(conv_par.shape),
                whole(head_vals.shape),
                whole(skip.shape),
                whole(spread.shape),
                whole(gather.shape),
                pl.BlockSpec((BLOCK, width), at),
                pl.BlockSpec((weight.shape[0], width), lambda step, me_ref: (0, 0)),
                whole(weight.shape),
            ],
            out_specs=[
                pl.BlockSpec((BLOCK, width + pre_width), at),
                pl.BlockSpec((BLOCK, weight.shape[0]), parted),
                whole((8, conv_width)),
                whole((8, LANES)),
                whole((8, width)),
            ],
            scratch_shapes=[
                pltpu.VMEM((state_size, width), F32),
                pltpu.VMEM((BLOCK + 8, conv_width), F32),
                pltpu.VMEM((BLOCK + 8, conv_width), F32),
            ],
        ),
        compiler_params=params(),
        cost_estimate=pl.CostEstimate(
            flops=total * width, bytes_accessed=total * width, transcendentals=0,
        ),
        name="scan_backward",
    )(me, dy, y, pre, pre, kept, conv_par, head_vals, skip, spread, gather, dz, gate_weight, weight)


def root_kernel(rows_ref, root_ref):
    vals = rows_ref[...]
    root_ref[...] = lax.rsqrt(jnp.mean(vals * vals, axis=1, keepdims=True) + NORM_EPS)


def first_root(rows):
    return pl.pallas_call(
        root_kernel,
        out_shape=jax.ShapeDtypeStruct((rows.shape[0], 1), F32),
        compiler_params=pltpu.CompilerParams(vmem_limit_bytes=VMEM_BYTES),
        cost_estimate=pl.CostEstimate(flops=10**11, bytes_accessed=rows.size * 4, transcendentals=0),
        name="first_root",
    )(rows)


def swap(vals, distance, count):
    return lax.ppermute(vals, "tensor", [(src, src ^ distance) for src in range(count)])


def gather_pieces(own, count):
    far = swap(own, 2, count)
    return [own, far, swap(own, 1, count), swap(far, 1, count)]


def gather_slots(own, count, beside=None):
    far = swap(own, 2, count)
    if beside is not None:
        far, beside = lax.optimization_barrier((far, beside))
    full = jnp.concatenate([own, far, swap(own, 1, count), swap(far, 1, count)], axis=0)
    return full if beside is None else (full, beside)


def gather_parts(parts, kept, count):
    parts = list(parts)
    gathered = []
    for spot, part in enumerate(parts):
        far = swap(part, 2, count)
        if spot + 1 < len(parts):
            far, parts[spot + 1] = lax.optimization_barrier((far, parts[spot + 1]))
        gathered.append([kept[spot], far, swap(part, 1, count), swap(far, 1, count)])
    return jnp.concatenate([part[spot] for spot in range(count) for part in gathered], axis=0)


def reduce_slots(sent, held, count, wire):
    return reduce_far(reduce_near(sent, held, count, wire), count, wire)


def reduce_near(sent, held, count, wire):
    return held.astype(F32) + swap(sent.astype(wire), 1, count).astype(F32)


def reduce_far(near, count, wire):
    return add_far(near, swap_far(near, count, wire))


def swap_far(near, count, wire):
    return swap(near[near.shape[0] // 2 :].astype(wire), 2, count)


def add_far(near, far):
    return near[: far.shape[0]] + far.astype(F32)


def ring_index(place, count):
    return jnp.where(place < count // 2, 2 * place, 2 * (count - place) - 1)


def ring_place(index, count):
    return jnp.where(index % 2 == 0, index // 2, count - (index + 1) // 2)


def ring_step(vals, way, count):
    order = list(range(0, count, 2)) + list(range(count - 1, 0, -2))
    pairs = [(order[spot], order[(spot + way) % count]) for spot in range(count)]
    return lax.ppermute(vals, "dp", pairs)


class RingReduce:
    def __init__(self, vals, count):
        self.vals, self.count = vals, count
        self.share = vals.shape[0] // count
        self.place = ring_place(lax.axis_index("dp"), count)
        self.total_hops = count // 2
        self.hops = {1: count // 2, -1: count - 1 - count // 2}
        self.moving = {way: self.chunk(way * hops).astype(LOW) for way, hops in self.hops.items()}
        self.done = 0

    def chunk(self, offset):
        index = ring_index((self.place + offset) % self.count, self.count)
        return lax.dynamic_slice_in_dim(self.vals, index * self.share, self.share, 0).astype(F32)

    def hop(self):
        self.done += 1
        for way, hops in self.hops.items():
            if self.done > hops:
                continue
            moved = ring_step(self.moving[way], way, self.count)
            if self.done < hops:
                moved = (moved.astype(F32) + self.chunk(way * (hops - self.done))).astype(LOW)
            self.moving[way] = moved

    def finish(self):
        while self.done < self.total_hops:
            self.hop()
        return self.chunk(0) + self.moving[1].astype(F32) + self.moving[-1].astype(F32)


def xor_step(vals, axis, distance, count):
    return lax.ppermute(vals, axis, [(src, src ^ distance) for src in range(count)])


def xor_sum(vals, axis, count):
    distance = 1
    while distance < count:
        vals = vals + xor_step(vals, axis, distance, count)
        distance *= 2
    return vals


def xor_gather(own, dp_count, tensor_count):
    stack = own
    for axis, count in (("dp", dp_count), ("tensor", tensor_count)):
        distance = 1
        while distance < count:
            stack = jnp.concatenate([stack, xor_step(stack, axis, distance, count)], axis=0)
            distance *= 2
    total = dp_count * tensor_count
    spots = jnp.arange(total)
    owner = (lax.axis_index("dp") ^ (spots % dp_count)) * tensor_count + (
        lax.axis_index("tensor") ^ (spots // dp_count)
    )
    chosen = owner[None, :] == spots[:, None]
    return jnp.sum(jnp.where(chosen[:, :, None], stack[None], 0.0), axis=1)


def adam_update(current, gradient, moment_old, square_old, step_rate, decay_coef):
    moment_new = BETA_ONE * moment_old + (1.0 - BETA_ONE) * gradient
    square_new = BETA_TWO * square_old + (1.0 - BETA_TWO) * gradient * gradient
    moment_hat = moment_new / (1.0 - BETA_ONE**STEP)
    square_hat = square_new / (1.0 - BETA_TWO**STEP)
    updated = current - step_rate * (
        moment_hat / (jnp.sqrt(square_hat) + ADAM_EPS) + decay_coef * current
    )
    return (updated, moment_new, square_new)


def inv_rms(vals):
    return lax.rsqrt(jnp.mean(vals * vals, axis=1, keepdims=True) + NORM_EPS)


def pad_rows(vals, rows):
    return jnp.pad(vals, ((0, rows - vals.shape[0]), (0, 0)))


def pad_lanes(vals, lanes):
    return jnp.pad(vals, ((0, 0), (0, lanes - vals.shape[1])))


def local(
    dp_count,
    tensor_count,
    resid_in,
    cotangent,
    w_zx,
    w_bc,
    w_dt,
    w_out,
    chan_par,
    head_par,
    bc_par,
    norm_gain,
    zx_first,
    zx_second,
    bc_first,
    bc_second,
    dt_first,
    dt_second,
    out_first,
    out_second,
    chan_first,
    chan_second,
    head_first,
    head_second,
    bcpar_first,
    bcpar_second,
    gain_first,
    gain_second,
):
    layer_total, depth_share, _, width = w_zx.shape
    rows_own, depth = resid_in.shape
    head_count = w_dt.shape[2]
    state_two = w_bc.shape[2]
    conv_width = width + state_two
    tap_total = bc_par.shape[1]
    pieces = rows_own // BLOCK
    me_dp = lax.axis_index("dp")
    me_tensor = lax.axis_index("tensor")
    me = me_tensor.astype(jnp.int32).reshape((1,))
    place = me_dp * tensor_count + me_tensor

    gain_share, bcpar_share = norm_gain.shape[1], bc_par.shape[2]
    flat = jnp.concatenate([norm_gain.reshape(-1), bc_par.reshape(-1)])[None, :]
    bc_weights = lax.all_gather(w_bc.astype(LOW), "tensor", axis=1, tiled=True)
    bc_weights, opening = lax.optimization_barrier((bc_weights, resid_in))
    flat, opening = lax.optimization_barrier((flat, first_root(opening)))
    weights = []
    for layer in range(layer_total):
        scan_share = jnp.concatenate(
            [
                w_zx[layer, :, 1, :].astype(LOW),
                bc_weights[layer],
                pad_lanes(w_dt[layer].astype(LOW), LANES),
            ],
            axis=1,
        )
        gate_share = jnp.concatenate(
            [w_zx[layer, :, 0, :].astype(LOW), w_out[layer].T.astype(LOW)], axis=1
        )
        if layer == 0:
            small = xor_gather(flat, dp_count, tensor_count)
        scan_weight = lax.all_gather(scan_share, "dp", axis=0, tiled=True)
        gate_weight = lax.all_gather(gate_share, "dp", axis=0, tiled=True)
        weights.append((scan_weight, gate_weight))
    gain_len = layer_total * gain_share
    gain_all = small[:, :gain_len].reshape(-1, layer_total, gain_share)
    gain_all = gain_all.transpose(1, 0, 2).reshape(layer_total, depth)
    bcpar_all = small[:, gain_len:].reshape(-1, layer_total, tap_total, bcpar_share)
    bcpar_all = bcpar_all.transpose(1, 2, 0, 3).reshape(layer_total, tap_total, state_two)

    spread = spread_matrix(head_count, width)
    def in_parts(vals):
        return [vals[part * BLOCK : (part + 1) * BLOCK] for part in range(pieces)]

    def in_turn(far_list, make):
        made, ready = [], []
        for spot, far in enumerate(far_list):
            if spot:
                far, held = lax.optimization_barrier((far, made[-1][0]))
                ready.append(held)
            made.append(make(spot, far))
        ready.append(made[-1][0])
        return made, ready

    hidden = in_parts(resid_in)
    roots = in_parts(opening)
    low_rows = ready_rows = None
    kept = []
    for layer in range(layer_total):
        scan_weight, gate_weight = weights[layer]
        conv_par = pad_rows(jnp.concatenate([chan_par[layer, :-1], bcpar_all[layer]], axis=1), 8)
        decay = -jnp.exp(head_par[layer, 1])
        head_vals = pad_rows(
            pad_lanes(jnp.stack([head_par[layer, 0], decay * LOG2E, decay], 0), LANES), 8
        )
        skip = pad_rows(jnp.repeat(head_par[layer, 2], HEAD_WIDTH)[None, :], 8)
        gain_q = chan_par[layer, -1:]
        if layer == 0:
            normed = (resid_in * opening * gain_all[layer][None, :]).astype(LOW)
            rows, scan_weight = gather_slots(normed, tensor_count, scan_weight)
            weights[0] = (scan_weight, gate_weight)
            rows, first_grad = lax.optimization_barrier((rows, cotangent.astype(LOW)))
            first_far = swap(first_grad, 2, tensor_count)
        else:
            rows = gather_parts(low_rows, ready_rows, tensor_count)
        pre, y, states = scan_forward(
            me, rows, scan_weight, conv_par, head_vals, skip, spread, pieces, 0.1 if layer else 8.0
        )
        if layer == 0:
            y, first_far = lax.optimization_barrier((y, first_far))
            first_full = jnp.concatenate(
                [first_grad, first_far, swap(first_grad, 1, tensor_count), swap(first_far, 1, tensor_count)], axis=0
            )
            y, first_full = lax.optimization_barrier((y, first_full))
        gate_z = None
        near_list, square_list = [], []
        for part in range(pieces):
            gate_z, sent, held, squares = gate_forward(rows, y, gate_weight, gain_q, gate_z, part, pieces)
            near_list.append(reduce_near(sent, held, tensor_count, LOW))
            square_list.append(squares)
        middle = square_list[0].shape[0] // 2
        square_sent = jnp.concatenate(
            [vals[middle + spot : middle + spot + BLOCK] for spot in range(0, middle, BLOCK) for vals in square_list]
        )
        square_held = jnp.concatenate(
            [vals[spot : spot + BLOCK] for spot in range(0, middle, BLOCK) for vals in square_list]
        )
        square_own = reduce_slots(square_sent, square_held, tensor_count, F32)
        near_list, square_own = lax.optimization_barrier((near_list, square_own))
        inv_list = in_parts(lax.rsqrt(square_own / INNER + NORM_EPS))
        far_list = [swap_far(near, tensor_count, LOW) for near in near_list]
        next_gain = gain_all[min(layer + 1, layer_total - 1)][None, :]

        def next_rows(spot, far, near_list=near_list, inv_list=inv_list, hidden=hidden, next_gain=next_gain):
            branch = add_far(near_list[spot], far)
            out = hidden[spot] + inv_list[spot] * branch
            root = inv_rms(out)
            return (out * root * next_gain).astype(LOW), out, root, branch

        made, ready_rows = in_turn(far_list, next_rows)
        kept.append(
            (
                hidden, roots, rows, pre, y, states, gate_z, inv_list, [entry[3] for entry in made],
                conv_par, head_vals, skip, gain_q,
            )
        )
        low_rows = [entry[0] for entry in made]
        hidden = [entry[1] for entry in made]
        roots = [entry[2] for entry in made]

    grad_hidden = in_parts(cotangent)
    zx_list = [None] * layer_total
    dt_list = [None] * layer_total
    out_list = [None] * layer_total
    bc_list = [None] * layer_total
    small_list = [None] * layer_total
    shared_list = [None] * layer_total
    gain_list = [None] * layer_total
    def place_scan(layer, total):
        z_sum, scan_sum = total[:, :width], total[:, width:]
        zx_list[layer] = jnp.stack([z_sum, scan_sum[:, :width]], axis=1)
        share = depth_share // tensor_count
        parts = [
            lax.dynamic_slice_in_dim(scan_sum[:, width:conv_width], (me_tensor ^ slot) * share, share, 0)
            for slot in [*range(0, tensor_count, 2), *range(1, tensor_count, 2)]
        ]
        middle = tensor_count // 2
        bc_list[layer] = reduce_slots(
            jnp.concatenate(parts[middle:], axis=0), jnp.concatenate(parts[:middle], axis=0), tensor_count, F32
        )
        dt_list[layer] = scan_sum[:, conv_width : conv_width + head_count]

    late = ()

    def owned(grad):
        return lax.psum_scatter(grad, "dp", scatter_dimension=0, tiled=True)

    for layer in reversed(range(layer_total)):
        scan_weight, gate_weight = weights[layer]
        (
            entering, roots, rows, pre, y, states, gate_z, inv_list, projected, conv_par, head_vals, skip, gain_q,
        ) = kept[layer]
        if layer == layer_total - 1:
            branch_low = [part.astype(LOW) for part in grad_hidden]
        stats = [
            jnp.concatenate([inv, jnp.sum(low.astype(F32) * branch, axis=1, keepdims=True)], axis=1)
            for inv, low, branch in zip(inv_list, branch_low, projected)
        ]
        stats = gather_slots(jnp.concatenate(stats, axis=0), tensor_count)
        full_grad = first_full if layer == layer_total - 1 else gather_parts(branch_low, ready_low, tensor_count)
        dz, dy, scaled, gain_five = gate_backward(full_grad, y, gate_z, stats, gate_weight, gain_q)
        out_grad = dot(full_grad, scaled, 0, 0).astype(LOW)
        dy, out_grad = lax.optimization_barrier((dy, out_grad))
        if layer + 1 < layer_total:
            late, out_grad = lax.optimization_barrier((late, out_grad))
        out_sum = owned(out_grad)
        dmerged, dnormed, conv_grad, head_grad, skip_grad = scan_backward(
            me, dy, y, pre, states, conv_par, head_vals, skip, spread, dz, gate_weight, scan_weight, pieces
        )
        out_sum, dnormed, dmerged = lax.optimization_barrier((out_sum, dnormed, dmerged))
        part_rows = dnormed.shape[0] // pieces
        near_list = []
        for part in range(pieces):
            vals = dnormed[part * part_rows : (part + 1) * part_rows]
            near_list.append(
                reduce_near(vals[part_rows // 2 :], vals[: part_rows // 2], tensor_count, LOW)
            )
        merged_grad = dot(rows, dmerged, 0, 0)
        if layer == 0:
            near_list, merged_grad = lax.optimization_barrier((near_list, merged_grad))
        far_list = [swap_far(near, tensor_count, LOW) for near in near_list]
        if layer == 0:
            ring = RingReduce(merged_grad, dp_count)
            for hop in range(1, ring.total_hops):
                ring.hop()
                if hop == 2:
                    ring.moving, far_list = lax.optimization_barrier((ring.moving, far_list))
            rest = (conv_grad, head_grad, skip_grad, gain_five, out_sum, late, far_list)
            ring.moving, rest = lax.optimization_barrier((ring.moving, rest))
            conv_grad, head_grad, skip_grad, gain_five, out_sum, late, far_list = rest
            if layer + 1 < layer_total:
                place_scan(layer + 1, late.astype(F32))
            place_scan(layer, ring.finish())
        else:
            far_list[-1], merged_grad = lax.optimization_barrier((far_list[-1], merged_grad.astype(LOW)))
            late = owned(merged_grad)
        out_list[layer] = out_sum.astype(F32).T
        gain = gain_all[layer][None, :]

        def next_grad(
            spot, far, near_list=near_list, entering=entering, roots=roots, grad_hidden=grad_hidden, gain=gain
        ):
            part_grad = add_far(near_list[spot], far)
            part_in, root = entering[spot], roots[spot]
            gained = part_grad * gain
            shift = jnp.mean(gained * part_in, axis=1, keepdims=True) * root * root * root
            out = grad_hidden[spot] + root * gained - part_in * shift
            return out.astype(LOW), out, jnp.sum(part_grad * part_in * root, axis=0)

        made, ready_low = in_turn(far_list, next_grad)
        branch_low = [entry[0] for entry in made]
        grad_hidden = [entry[1] for entry in made]
        gain_grad = sum(entry[2] for entry in made)

        chan_grad = jnp.concatenate([conv_grad[:5, :width], gain_five], axis=0)
        skip_sum = skip_grad[0].reshape(head_count, HEAD_WIDTH).sum(axis=1)
        head_all = jnp.concatenate(
            [head_grad[0, :head_count], head_grad[1, :head_count], skip_sum]
        )
        small_list[layer] = jnp.concatenate([chan_grad.reshape(-1), head_all])
        gain_list[layer] = gain_grad
        shared_list[layer] = conv_grad[:5, width:].reshape(-1)

    shared = xor_sum(jnp.stack(shared_list, 0), "tensor", tensor_count)
    both = xor_sum(jnp.concatenate([jnp.stack(small_list, 0), shared], axis=1), "dp", dp_count)
    chan_len = chan_par.shape[1] * width
    head_len = head_par.shape[1] * head_count
    chan_stack = both[:, :chan_len].reshape(chan_par.shape)
    head_stack = both[:, chan_len : chan_len + head_len].reshape(head_par.shape)
    shared = both[:, chan_len + head_len :]
    gains = xor_sum(xor_sum(jnp.stack(gain_list, 0), "tensor", tensor_count), "dp", dp_count)
    gain_stack = lax.dynamic_slice_in_dim(gains, place * gain_share, gain_share, axis=1)
    bcpar_stack = lax.dynamic_slice_in_dim(
        shared.reshape(layer_total, tap_total, state_two), place * bcpar_share, bcpar_share, axis=2
    )

    zx_stack = with_layout_constraint(jnp.stack(zx_list, 0), Layout((0, 1, 2, 3)))
    zx_new = adam_update(w_zx, zx_stack, zx_first, zx_second, MATRIX_RATE, MATRIX_DECAY)
    bc_new = adam_update(w_bc, jnp.stack(bc_list, 0), bc_first, bc_second, MATRIX_RATE, MATRIX_DECAY)
    dt_new = adam_update(w_dt, jnp.stack(dt_list, 0), dt_first, dt_second, MATRIX_RATE, MATRIX_DECAY)
    out_new = adam_update(w_out, jnp.stack(out_list, 0), out_first, out_second, MATRIX_RATE, MATRIX_DECAY)
    chan_new = adam_update(chan_par, chan_stack, chan_first, chan_second, SMALL_RATE, 0.0)
    head_new = adam_update(head_par, head_stack, head_first, head_second, HEAD_RATE, 0.0)
    bcpar_new = adam_update(bc_par, bcpar_stack, bcpar_first, bcpar_second, SMALL_RATE, 0.0)
    gain_new = adam_update(norm_gain, gain_stack, gain_first, gain_second, SMALL_RATE, 0.0)
    return (
        jnp.concatenate(hidden, axis=0), jnp.concatenate(grad_hidden, axis=0), *zx_new, *bc_new, *dt_new, *out_new, *chan_new, *head_new, *bcpar_new, *gain_new,
    )


def solution(mesh):
    in_specs = (
        P(("dp", "tensor"), None),
        P(("dp", "tensor"), None),
        P(None, "dp", None, "tensor"),
        P(None, ("dp", "tensor"), None),
        P(None, "dp", "tensor"),
        P(None, "tensor", "dp"),
        P(None, None, "tensor"),
        P(None, None, "tensor"),
        P(None, None, ("dp", "tensor")),
        P(None, ("dp", "tensor")),
        P(None, "dp", None, "tensor"),
        P(None, "dp", None, "tensor"),
        P(None, ("dp", "tensor"), None),
        P(None, ("dp", "tensor"), None),
        P(None, "dp", "tensor"),
        P(None, "dp", "tensor"),
        P(None, "tensor", "dp"),
        P(None, "tensor", "dp"),
        P(None, None, "tensor"),
        P(None, None, "tensor"),
        P(None, None, "tensor"),
        P(None, None, "tensor"),
        P(None, None, ("dp", "tensor")),
        P(None, None, ("dp", "tensor")),
        P(None, ("dp", "tensor")),
        P(None, ("dp", "tensor")),
    )
    out_specs = (
        P(("dp", "tensor"), None),
        P(("dp", "tensor"), None),
        P(None, "dp", None, "tensor"),
        P(None, "dp", None, "tensor"),
        P(None, "dp", None, "tensor"),
        P(None, ("dp", "tensor"), None),
        P(None, ("dp", "tensor"), None),
        P(None, ("dp", "tensor"), None),
        P(None, "dp", "tensor"),
        P(None, "dp", "tensor"),
        P(None, "dp", "tensor"),
        P(None, "tensor", "dp"),
        P(None, "tensor", "dp"),
        P(None, "tensor", "dp"),
        P(None, None, "tensor"),
        P(None, None, "tensor"),
        P(None, None, "tensor"),
        P(None, None, "tensor"),
        P(None, None, "tensor"),
        P(None, None, "tensor"),
        P(None, None, ("dp", "tensor")),
        P(None, None, ("dp", "tensor")),
        P(None, None, ("dp", "tensor")),
        P(None, ("dp", "tensor")),
        P(None, ("dp", "tensor")),
        P(None, ("dp", "tensor")),
    )
    return jax.shard_map(
        functools.partial(local, mesh.shape["dp"], mesh.shape["tensor"]), mesh=mesh, in_specs=in_specs, out_specs=out_specs, check_vma=False)
```
